32 devices in a mesh: section: 16 (over z, y, core), tensor: 2 (over x).
Axes of the slice: x: 2, y: 2, z: 4, core: 2. Of those that a mesh axis runs over, the one named last changes fastest.
Arguments:
- memory: bfloat16 [2, 12288, 4096], P(None, 'section', 'tensor'), may hold values from -4 to 4
- queries: bfloat16 [4096, 4096], P(('section', 'tensor')), may hold values from -6.5 to 6.5
- out_grad: bfloat16 [4096, 4096], P(('section', 'tensor')), may hold values from -6 to 6
- enc_lengths: int32 [16, 8], replicated, may hold values from 1 to 128, 768 in all within a row
- dec_lengths: int32 [16, 8], replicated, may hold values from 1 to 64, 256 in all within a row
- readers: int32 [16, 8], replicated, may hold values from 0 to 15, as said below
Outputs:
- attended: bfloat16 [4096, 4096], P(('section', 'tensor'))
- query_grad: bfloat16 [4096, 4096], P(('section', 'tensor'))
- memory_grad: bfloat16 [2, 12288, 4096], P(None, 'section', 'tensor')
The draws below stay inside these ranges and needn't reach their ends.
Inputs may be any that keep to these rules, and one draw needn't show every extreme that they name: `readers`: the reader of example j of encoder device s is (s + k * 2 + 1) modulo 16 for some k < 8; each encoder device names each of its 8 such devices exactly 1 times, so every decoder device is named exactly 8 times.
All inputs are finite; a program needn't handle non-finite values.
Results may differ from the reference program's by a relative error of at most 0.011.
Values may be sent and summed in bfloat16 or wider, within the bound.
A program may use at most 64 MiB of HBM per device.

```python
import math
import jax
import jax.numpy as jnp
import numpy as np
from jax import lax

HEADS = 32
HD = 128
EX_DEV = 8
ENC_MAX = 128
DEC_MAX = 64
PARTNERS = 8
ENC_DEV = 768
DEC_DEV = 256
ENC_TOKENS = 12288
DEC_TOKENS = 4096
N_SECTION = 16


def draw_memory(key, part):
    row_total = ENC_DEV * N_SECTION
    feature_width = HEADS * HD
    key_base = jax.random.fold_in(key, 0)
    baseline = jax.random.normal(key_base, (2, row_total, feature_width), jnp.float32)
    return jnp.clip(baseline, -4.0, 4.0).astype(jnp.bfloat16)


def draw_queries(key, part):
    row_total = DEC_DEV * N_SECTION
    feature_width = HEADS * HD
    key_base = jax.random.fold_in(key, 0)
    baseline = jax.random.normal(key_base, (row_total, feature_width), jnp.float32)
    return jnp.clip(baseline, -4.0, 4.0).astype(jnp.bfloat16)


def draw_readers(key, part):
    spacing = N_SECTION // PARTNERS
    order_keys = jax.random.split(key, N_SECTION)
    slot_order = jax.vmap(lambda single: jax.random.permutation(single, EX_DEV))(order_keys).astype(jnp.int32)
    partner_index = slot_order % PARTNERS
    holders = jnp.arange(N_SECTION, dtype=jnp.int32)[:, None]
    return ((holders + partner_index * spacing + 1) % N_SECTION).astype(jnp.int32)


def level_of(own_key, extent, cuts, low, largest):
    loudness, own = 1.0, jax.random.fold_in(own_key, 6)
    for dim, shards_of in cuts:
        heights = jnp.exp(jax.random.uniform(jax.random.fold_in(own, dim), (shards_of,), jnp.float32, low / len(cuts), largest / len(cuts)))
        loudness = loudness * jnp.repeat(heights, extent[dim] // shards_of).reshape([-1 if axis == dim else 1 for axis in range(len(extent))])
    return loudness


def length_profile(count, total, limit, skew):
    portions = [(1 << 20) // math.isqrt(grade ** skew) + 1 for grade in range(2, count + 1)]
    rest, given = total - limit - (count - 1), [1] * (count - 1)
    while rest > 0:
        movable = [i for i in range(count - 1) if given[i] < limit]
        pool, left = sum([portions[i] for i in movable]), rest
        for i in movable:
            more = min(limit - given[i], max(1, left * portions[i] // pool), rest)
            given[i] = given[i] + more
            rest = rest - more
    return np.array([limit] + given)


def uneven(own_key, count, total, limit, skew):
    if count == 2:
        one = jax.random.randint(own_key, (), max(1, total - limit), min(limit, total - 1) + 1)
        return jnp.stack([one, total - one])
    sizes = jnp.asarray(length_profile(count, total, limit, skew), jnp.int32)
    twos = (count - 1) // 2
    donor, receiver = sizes[1:1 + 2 * twos:2], sizes[2:2 + 2 * twos:2]
    margin = jnp.minimum(donor - 1, limit - receiver)
    shifted = jax.random.randint(jax.random.fold_in(own_key, 1), (twos,), 0, 1 << 20) % (margin + 1)
    sizes = sizes.at[1:1 + 2 * twos:2].set(donor - shifted).at[2:2 + 2 * twos:2].set(receiver + shifted)
    return sizes[jax.random.permutation(jax.random.fold_in(own_key, 2), count)]


def gaussian(stream_key, shape, spread, most, pieces=(), kind=jnp.bfloat16):
    drawn = spread * jax.random.normal(stream_key, shape, jnp.float32)
    if pieces:
        drawn = drawn * level_of(stream_key, shape, pieces, -0.22, 0.18)
    return jnp.clip(drawn, -most, most).astype(kind)


def setup_inputs(seed: int = 0) -> dict:
    streams_of = jax.random.split(jax.random.key(seed), 7)
    memory = draw_memory(jax.random.fold_in(streams_of[6], 71), 0)
    queries = draw_queries(jax.random.fold_in(streams_of[6], 71), 0)
    out_grad = gaussian(streams_of[2], (DEC_TOKENS, HEADS * HD), 1.0, 6.0, ((0, 32),))
    enc_lengths = jax.vmap(lambda own: uneven(own, EX_DEV, ENC_DEV, ENC_MAX, 2))(jax.random.split(streams_of[3], N_SECTION)).reshape((N_SECTION, EX_DEV)).astype(jnp.int32)
    dec_lengths = jax.vmap(lambda own: uneven(own, EX_DEV, DEC_DEV, DEC_MAX, 1))(jax.random.split(streams_of[4], N_SECTION)).reshape((N_SECTION, EX_DEV)).astype(jnp.int32)
    readers = draw_readers(jax.random.fold_in(streams_of[6], 71), 0)
    return dict(memory=memory, queries=queries, out_grad=out_grad, enc_lengths=enc_lengths, dec_lengths=dec_lengths, readers=readers)


def reference(memory, queries, out_grad, enc_lengths, dec_lengths, readers):
    feature_width = HEADS * HD
    scaling = HD ** -0.5
    flattened = readers.reshape(-1).astype(jnp.int32)
    everyone = jnp.arange(flattened.shape[0], dtype=jnp.int32)
    enc_bounds = jnp.cumsum(enc_lengths, axis=1).astype(jnp.int32)
    device_base = jnp.arange(N_SECTION, dtype=jnp.int32)[:, None] * ENC_DEV
    enc_start = (enc_bounds - enc_lengths + device_base).reshape(-1).astype(jnp.int32)
    enc_sizes = enc_lengths.reshape(-1).astype(jnp.int32)
    key_offsets = jnp.arange(ENC_MAX, dtype=jnp.int32)
    dec_offsets = jnp.arange(DEC_MAX, dtype=jnp.int32)
    labels = jnp.arange(EX_DEV, dtype=jnp.int32)
    positions = jnp.arange(DEC_DEV, dtype=jnp.int32)

    def per_reader(carry, reader):
        key_acc, value_acc = carry
        is_mine = (flattened == reader).astype(jnp.int32)
        ordinal = (jnp.cumsum(is_mine) - is_mine).astype(jnp.int32)
        matches = (is_mine[None, :] == 1) & (ordinal[None, :] == labels[:, None])
        example_ids = jnp.sum(jnp.where(matches, everyone[None, :], 0), axis=1).astype(jnp.int32)
        begins = enc_start[example_ids]
        sizes = enc_sizes[example_ids]
        key_valid = key_offsets[None, :] < sizes[:, None]
        key_rows = jnp.where(key_valid, begins[:, None] + key_offsets[None, :], 0).astype(jnp.int32)
        dec_row = lax.dynamic_index_in_dim(dec_lengths, reader, 0, keepdims=False).astype(jnp.int32)
        dec_bounds = jnp.cumsum(dec_row).astype(jnp.int32)
        dec_begin = (dec_bounds - dec_row).astype(jnp.int32)
        dec_valid = dec_offsets[None, :] < dec_row[:, None]
        dec_rows = jnp.where(dec_valid, reader * DEC_DEV + dec_begin[:, None] + dec_offsets[None, :], 0).astype(jnp.int32)
        block_shape = (EX_DEV, DEC_MAX, HEADS, HD)
        query_block = jnp.where(dec_valid[:, :, None], queries[dec_rows], 0).astype(jnp.float32).reshape(block_shape)
        grad_block = jnp.where(dec_valid[:, :, None], out_grad[dec_rows], 0).astype(jnp.float32).reshape(block_shape)
        key_block = memory[0][key_rows].astype(jnp.float32).reshape(EX_DEV, ENC_MAX, HEADS, HD)
        value_block = memory[1][key_rows].astype(jnp.float32).reshape(EX_DEV, ENC_MAX, HEADS, HD)
        scores = jnp.einsum("eqhd,ekhd->ehqk", query_block, key_block) * scaling
        scores = jnp.where(key_valid[:, None, None, :], scores, -jnp.inf)
        highest = jnp.max(scores, axis=3, keepdims=True)
        weights = jnp.exp(scores - highest)
        probabilities = weights / jnp.sum(weights, axis=3, keepdims=True)
        probs_low = lax.optimization_barrier(probabilities.astype(jnp.bfloat16)).astype(jnp.float32)
        attended = jnp.einsum("ehqk,ekhd->eqhd", probs_low, value_block).astype(jnp.bfloat16).reshape(EX_DEV * DEC_MAX, feature_width)
        dprobs = jnp.einsum("eqhd,ekhd->ehqk", grad_block, value_block)
        row_delta = jnp.sum(probabilities * dprobs, axis=3, keepdims=True)
        dscores = lax.optimization_barrier((probabilities * (dprobs - row_delta)).astype(jnp.bfloat16)).astype(jnp.float32)
        query_grad = (jnp.einsum("ehqk,ekhd->eqhd", dscores, key_block) * scaling).astype(jnp.bfloat16).reshape(EX_DEV * DEC_MAX, feature_width)
        key_terms = (jnp.einsum("ehqk,eqhd->ekhd", dscores, query_block) * scaling).astype(jnp.bfloat16).reshape(-1, feature_width)
        value_terms = jnp.einsum("ehqk,eqhd->ekhd", probs_low, grad_block).astype(jnp.bfloat16).reshape(-1, feature_width)
        flat_valid = key_valid.reshape(-1, 1)
        flat_rows = key_rows.reshape(-1)
        key_acc = key_acc.at[flat_rows].add(jnp.where(flat_valid, key_terms, jnp.zeros((), key_terms.dtype)))
        value_acc = value_acc.at[flat_rows].add(jnp.where(flat_valid, value_terms, jnp.zeros((), value_terms.dtype)))
        member = jnp.sum((positions[:, None] >= dec_bounds[None, :]).astype(jnp.int32), axis=1).astype(jnp.int32)
        token_index = (member * DEC_MAX + positions - dec_begin[member]).astype(jnp.int32)
        return (key_acc, value_acc), (attended[token_index], query_grad[token_index])

    zero_acc = jnp.zeros((ENC_TOKENS, feature_width), jnp.bfloat16)
    (key_acc, value_acc), (attended, query_grad) = lax.scan(per_reader, (zero_acc, zero_acc), jnp.arange(N_SECTION, dtype=jnp.int32))
    memory_grad = jnp.stack([key_acc, value_acc])
    return attended.reshape(-1, feature_width), query_grad.reshape(-1, feature_width), memory_grad
```

```python
import functools

import jax
import jax.numpy as jnp
import numpy as np
from jax import lax
from jax.experimental import pallas as pl
from jax.experimental.pallas import tpu as pltpu
from jax.sharding import PartitionSpec as P

HD = 128
ENC_MAX = 128
DEC_MAX = 64
PARTNERS = 8
MOST_CHUNKS = 8
BF16 = jnp.bfloat16
F32 = jnp.float32
MESH = pl.DeviceIdType.MESH


def matmul(a, b, dims):
    return lax.dot_general(a, b, (dims, ((), ())), preferred_element_type=F32)


NN = ((1,), (0,))
NT = ((1,), (1,))
TN = ((0,), (0,))


def chunk_count(width):
    return min(MOST_CHUNKS, width // HD)


def staged_kernel(sections, tensors, *refs):
    inputs, results, staging = refs[:6], refs[6:9], refs[9:12]
    sem = refs[-1]
    kernel(sections, tensors, *inputs, *staging, *refs[12:-1])
    copies = [
        pltpu.make_async_copy(source, target, sem.at[i])
        for i, (source, target) in enumerate(zip(staging, results))
    ]
    for copy in copies:
        copy.start()
    for copy in copies:
        copy.wait()


def kernel(
    sections,
    tensors,
    mem_hbm,
    q_hbm,
    g_hbm,
    enc_hbm,
    dec_hbm,
    readers_hbm,
    att_out,
    qg_out,
    mg_out,
    mem_v,
    dec_v,
    fsend,
    frecv,
    osend,
    oret,
    fin_v,
    kv_x,
    d_x,
    pack_m,
    unpack_m,
    enc_m,
    grad_m,
    enc_len,
    dec_len,
    readers,
    meta,
    a_send,
    a_recv,
    a_local,
    f_send,
    f_recv,
    o_send,
    o_recv,
    g_send,
    g_recv,
    g_local,
    m_in,
    s_in,
):
    me = lax.axis_index("section")
    mine = lax.axis_index("tensor")
    rows = q_hbm.shape[0]
    enc_count = mem_v.shape[1]
    dec_count = dec_v.shape[2]
    width = mem_v.shape[2]
    chunks = chunk_count(width)
    piece = width // chunks
    spacing = sections // PARTNERS
    scaling = HD ** (-0.5)

    def holder_of(slot):
        return lax.rem(me + 2 * sections - slot * spacing - 1, sections)

    def reader_of(slot):
        return lax.rem(me + slot * spacing + 1, sections)

    half = PARTNERS // 2

    def peer_of(step):
        return lax.rem(mine + step, tensors)

    mem_copy = pltpu.make_async_copy(mem_hbm, mem_v, m_in)
    scalar_copies = [
        pltpu.make_async_copy(source, target, s_in.at[i])
        for i, (source, target) in enumerate(
            ((enc_hbm, enc_len), (dec_hbm, dec_len), (readers_hbm, readers))
        )
    ]
    for copy in scalar_copies:
        copy.start()

    barrier = pltpu.get_barrier_semaphore()
    for step in range(1, tensors):
        pl.semaphore_signal(
            barrier, inc=1, device_id={"tensor": peer_of(step)}, device_id_type=MESH
        )
    for slot in range(PARTNERS):
        pl.semaphore_signal(
            barrier, inc=1, device_id={"section": holder_of(slot)}, device_id_type=MESH
        )
        pl.semaphore_signal(
            barrier, inc=1, device_id={"section": reader_of(slot)}, device_id_type=MESH
        )
    pl.semaphore_wait(barrier, tensors - 1 + 2 * PARTNERS)

    own_rows = pl.ds(pl.multiple_of(mine * rows, rows), rows)

    def first_copy(c, a, step):
        peer = peer_of(step)
        source = (q_hbm, g_hbm)[a]
        columns = pl.ds(pl.multiple_of(peer * width + c * piece, piece), piece)
        if step == 0:
            return pltpu.make_async_copy(
                source.at[:, columns], dec_v.at[c, a, own_rows], a_local.at[c, a]
            )
        return pltpu.make_async_remote_copy(
            src_ref=source.at[:, columns],
            dst_ref=dec_v.at[c, a, own_rows],
            send_sem=a_send.at[c, a, step - 1],
            recv_sem=a_recv.at[c, a, step - 1],
            device_id={"tensor": peer},
            device_id_type=MESH,
        )

    def fetch(c):
        for a in range(2):
            for step in list(range(1, tensors)) + [0]:
                first_copy(c, a, step).start()

    fetch(0)
    mem_copy.start()
    for copy in scalar_copies:
        copy.wait()

    start = jnp.int32(0)
    for i in range(PARTNERS):
        length = dec_len[i, me]
        meta[0, i] = start
        meta[1, i] = length
        start = start + length
    for slot in range(PARTNERS):
        reader = reader_of(slot)
        start, begin, size = jnp.int32(0), jnp.int32(0), jnp.int32(0)
        for j in range(PARTNERS):
            length = enc_len[j, me]
            match = readers[j, me] == reader
            begin = jnp.where(match, start, begin)
            size = jnp.where(match, length, size)
            start = start + length
        meta[2, slot] = begin
        meta[3, slot] = size

    def one_hot(hits):
        return jnp.where(hits, 1.0, 0.0).astype(BF16)

    def iota(shape, dim):
        return lax.broadcasted_iota(jnp.int32, shape, dim)

    for i in range(PARTNERS):
        shape = (DEC_MAX, dec_count)
        within = iota(shape, 0)
        hits = (iota(shape, 1) - within == meta[0, i]) & (within < meta[1, i])
        pack_m[i // half, (i % half) * DEC_MAX : (i % half + 1) * DEC_MAX, :] = one_hot(hits)

    def forward_copy(c, slot):
        holder = holder_of(slot)
        return pltpu.make_async_remote_copy(
            src_ref=fsend.at[c, :, lax.div(holder, spacing)],
            dst_ref=frecv.at[c, :, slot],
            send_sem=f_send.at[c, slot],
            recv_sem=f_recv.at[c, slot],
            device_id={"section": holder},
            device_id_type=MESH,
        )

    def back_copy(c, slot):
        return pltpu.make_async_remote_copy(
            src_ref=osend.at[c, :, slot],
            dst_ref=oret.at[c, :, lax.div(me, spacing)],
            send_sem=o_send.at[c, slot],
            recv_sem=o_recv.at[c, lax.div(me, spacing)],
            device_id={"section": reader_of(slot)},
            device_id_type=MESH,
        )

    def back_arrival(c, i):
        return pltpu.make_async_remote_copy(
            src_ref=osend.at[c, :, i],
            dst_ref=oret.at[c, :, i],
            send_sem=o_send.at[c, i],
            recv_sem=o_recv.at[c, i],
            device_id={"section": reader_of(i)},
            device_id_type=MESH,
        )

    def last_copy(c, a, step):
        peer = peer_of(step)
        target = (att_out, qg_out)[a]
        source = fin_v.at[c, a, pl.ds(pl.multiple_of(peer * rows, rows), rows)]
        columns = pl.ds(pl.multiple_of(mine * width + c * piece, piece), piece)
        if step == 0:
            return pltpu.make_async_copy(source, target.at[:, columns], g_local.at[c, a])
        return pltpu.make_async_remote_copy(
            src_ref=source,
            dst_ref=target.at[:, columns],
            send_sem=g_send.at[c, a, step - 1],
            recv_sem=g_recv.at[c, a, step - 1],
            device_id={"tensor": peer},
            device_id_type=MESH,
        )

    def pack(c):
        for a in range(2):
            first_copy(c, a, 0).wait()
            for step in range(1, tensors):
                first_copy(c, a, step).wait_recv()
        if c + 1 < chunks:
            fetch(c + 1)
        for a in range(2):
            for g in range(2):
                block = matmul(pack_m[g], dec_v[c, a], NN).astype(BF16)
                fsend[c, a, g * half : (g + 1) * half] = block.reshape(half, DEC_MAX, piece)

        @pl.loop(0, PARTNERS)
        def _(turn):
            forward_copy(c, turn).start()

    def expand(c):
        @pl.loop(0, PARTNERS // 2)
        def _(g):
            for a in range(2):
                block = matmul(enc_m[g], mem_v[a, :, c * piece : (c + 1) * piece], NN)
                kv_x[c, a, pl.ds(g * 2, 2)] = block.astype(BF16).reshape(2, ENC_MAX, piece)

    def attend(c):
        @pl.loop(0, PARTNERS)
        def _(turn):
            slot = turn
            forward_copy(c, slot).wait_recv()
            valid = iota((DEC_MAX, ENC_MAX), 1) < meta[3, slot]
            for h in range(piece // HD):
                at = slice(h * HD, (h + 1) * HD)
                q = frecv[c, 0, slot, :, at]
                g = frecv[c, 1, slot, :, at]
                k = kv_x[c, 0, slot, :, at]
                v = kv_x[c, 1, slot, :, at]
                scores = jnp.where(valid, matmul(q, k, NT) * scaling, -jnp.inf)
                weights = jnp.exp(scores - jnp.max(scores, axis=1, keepdims=True))
                probs = weights / jnp.sum(weights, axis=1, keepdims=True)
                low = probs.astype(BF16)
                dprobs = matmul(g, v, NT)
                delta = jnp.sum(probs * dprobs, axis=1, keepdims=True)
                dscores = (probs * (dprobs - delta)).astype(BF16)
                osend[c, 0, slot, :, at] = matmul(low, v, NN).astype(BF16)
                osend[c, 1, slot, :, at] = (matmul(dscores, k, NN) * scaling).astype(BF16)
                d_x[0, slot, :, at] = (matmul(dscores, q, TN) * scaling).astype(BF16)
                d_x[1, slot, :, at] = matmul(low, g, TN).astype(BF16)
            back_copy(c, slot).start()

    def collect(c):
        @pl.loop(0, enc_count // 256)
        def _(b):
            at = pl.ds(pl.multiple_of(b * 256, 256), 256)
            for a in range(2):
                block = d_x[a].reshape(PARTNERS * ENC_MAX, piece)
                mg_out[a, at, c * piece : (c + 1) * piece] = matmul(
                    grad_m[at, :], block, NN
                ).astype(BF16)

    def finish(c):
        @pl.loop(0, PARTNERS)
        def _(i):
            back_arrival(c, i).wait_recv()

        for a in range(2):
            block = oret[c, a].reshape(PARTNERS * DEC_MAX, piece)
            fin_v[c, a] = matmul(unpack_m[...], block, NN).astype(BF16)
            for step in list(range(1, tensors)) + [0]:
                last_copy(c, a, step).start()

    def settle():
        for c in range(chunks):
            for a in range(2):
                for step in range(1, tensors):
                    first_copy(c, a, step).wait_send()

            @pl.loop(0, PARTNERS)
            def _(slot):
                forward_copy(c, slot).wait_send()
                back_copy(c, slot).wait_send()

    pack(0)

    for slot in range(PARTNERS):
        shape = (ENC_MAX, enc_count)
        within = iota(shape, 0)
        hits = (iota(shape, 1) - within == meta[2, slot]) & (within < meta[3, slot])
        enc_m[slot // 2, (slot % 2) * ENC_MAX : (slot % 2 + 1) * ENC_MAX, :] = one_hot(hits)
    mem_copy.wait()
    expand(0)
    pack(1)

    position = iota((dec_count, 1), 0)
    goal = jnp.full((dec_count, 1), -1, jnp.int32)
    for i in range(PARTNERS):
        within = position - meta[0, i]
        goal = jnp.where((within >= 0) & (within < meta[1, i]), within + i * DEC_MAX, goal)
    unpack_m[...] = one_hot(iota((dec_count, PARTNERS * DEC_MAX), 1) == goal)
    for b in range(enc_count // 256):
        position = iota((256, 1), 0) + b * 256
        goal = jnp.full((256, 1), -1, jnp.int32)
        for slot in range(PARTNERS):
            within = position - meta[2, slot]
            goal = jnp.where(
                (within >= 0) & (within < meta[3, slot]), within + slot * ENC_MAX, goal
            )
        hits = iota((256, PARTNERS * ENC_MAX), 1) == goal
        grad_m[b * 256 : (b + 1) * 256, :] = one_hot(hits)

    expand(1)
    for c in range(2, chunks):
        pack(c)
        expand(c)
    for c in range(chunks):
        attend(c)
        collect(c)
        if c >= 3:
            finish(c - 3)
    for c in range(max(chunks - 3, 0), chunks):
        if c == chunks - 1:
            settle()
        finish(c)

    for c in range(chunks):
        for a in range(2):
            for step in range(1, tensors):
                last_copy(c, a, step).wait()
            last_copy(c, a, 0).wait()


def padded_body(sections, tensors, staged, memory, queries, out_grad, enc_lengths, dec_lengths, readers):
    enc_count, width = memory.shape[1:]
    rows = queries.shape[0]
    dec_count = rows * tensors
    chunks = chunk_count(width)
    piece = width // chunks
    blocks = (chunks, 2, PARTNERS, DEC_MAX, piece)
    peers = max(tensors - 1, 1)
    scalars = (enc_lengths.T, dec_lengths.T, readers.T)
    anywhere = pl.BlockSpec(memory_space=pl.ANY)
    resident = pl.BlockSpec(memory_space=pltpu.VMEM)
    results = [array.shape for array in (queries, queries, memory)]
    dma = pltpu.SemaphoreType.DMA
    return pl.pallas_call(
        functools.partial(staged_kernel if staged else kernel, sections, tensors),
        out_shape=tuple(
            jax.ShapeDtypeStruct(shape, BF16) if staged else pltpu.VMEM(shape, BF16)
            for shape in results
        ),
        in_specs=[anywhere] * 6,
        out_specs=(anywhere if staged else resident,) * 3,
        scratch_shapes=[
            *[pltpu.VMEM(shape, BF16) for shape in results if staged],
            pltpu.VMEM((2, enc_count, width), BF16),
            pltpu.VMEM((chunks, 2, dec_count, piece), BF16),
            pltpu.VMEM(blocks, BF16),
            pltpu.VMEM(blocks, BF16),
            pltpu.VMEM(blocks, BF16),
            pltpu.VMEM(blocks, BF16),
            pltpu.VMEM((chunks, 2, dec_count, piece), BF16),
            pltpu.VMEM((chunks, 2, PARTNERS, ENC_MAX, piece), BF16),
            pltpu.VMEM((2, PARTNERS, ENC_MAX, piece), BF16),
            pltpu.VMEM((2, PARTNERS // 2 * DEC_MAX, dec_count), BF16),
            pltpu.VMEM((dec_count, PARTNERS * DEC_MAX), BF16),
            pltpu.VMEM((PARTNERS // 2, 2 * ENC_MAX, enc_count), BF16),
            pltpu.VMEM((enc_count, PARTNERS * ENC_MAX), BF16),
            *[pltpu.SMEM(array.shape, jnp.int32) for array in scalars],
            pltpu.SMEM((4, PARTNERS), jnp.int32),
            dma((chunks, 2, peers)),
            dma((chunks, 2, peers)),
            dma((chunks, 2)),
            dma((chunks, PARTNERS)),
            dma((chunks, PARTNERS)),
            dma((chunks, PARTNERS)),
            dma((chunks, PARTNERS)),
            dma((chunks, 2, peers)),
            dma((chunks, 2, peers)),
            dma((chunks, 2)),
            dma,
            dma((3,)),
            *[dma((3,))] * staged,
        ],
        compiler_params=pltpu.CompilerParams(
            collective_id=0, has_side_effects=True, vmem_limit_bytes=(56 if staged else 46) * 1024 * 1024
        ),
    )(memory, queries, out_grad, *scalars)


ZS = 4
CAP = 640
RING = 4


def packed_kernel(
    mem_hbm,
    q_hbm,
    g_hbm,
    enc_hbm,
    dec_hbm,
    readers_hbm,
    att_out,
    qg_out,
    mg_out,
    own,
    inc,
    out,
    dsend,
    drecv,
    osend,
    oret,
    rin,
    rout,
    fin_v,
    mem_v,
    mg_v,
    mem_f,
    d_x,
    fwd_m,
    slot_m,
    ownslot_m,
    ret_m,
    fin_m,
    grad_m,
    enc_len,
    dec_len,
    readers,
    pre,
    seg,
    meta,
    a_send,
    a_recv,
    f_send,
    f_recv,
    d_send,
    d_recv,
    o_send,
    o_recv,
    r_send,
    r_recv,
    g_send,
    g_recv,
    m_in,
    m_out,
    s_in,
):
    me = lax.axis_index("section")
    x = lax.axis_index("tensor")
    z = lax.div(me, 4)
    y = lax.rem(lax.div(me, 2), 2)
    core = lax.rem(me, 2)
    rows = q_hbm.shape[0]
    dec_count = 2 * rows
    enc_count = mem_hbm.shape[1]
    width = mem_hbm.shape[2]
    half_width = width // 2
    chunks = half_width // HD
    cap = inc.shape[2]
    scaling = HD ** (-0.5)
    has_right = z < ZS - 1
    has_left = z > 0
    far = jnp.maximum(z, ZS - 1 - z)

    def flip(value, step):
        return lax.rem(value + step, 2)

    def section_of(zz, yy, cc):
        return zz * 4 + yy * 2 + cc

    def iota(shape, dim):
        return lax.broadcasted_iota(jnp.int32, shape, dim)

    def one_hot(hits):
        return jnp.where(hits, 1.0, 0.0).astype(BF16)

    scalar_copies = [
        pltpu.make_async_copy(source, target, s_in.at[i])
        for i, (source, target) in enumerate(
            ((enc_hbm, enc_len), (dec_hbm, dec_len), (readers_hbm, readers))
        )
    ]
    for copy in scalar_copies:
        copy.start()

    barrier = pltpu.get_barrier_semaphore()

    def greet(section, tensor):
        pl.semaphore_signal(
            barrier,
            inc=1,
            device_id={"section": section, "tensor": tensor},
            device_id_type=MESH,
        )

    greet(section_of(z, y, core), flip(x, 1))
    greet(section_of(z, y, flip(core, 1)), flip(x, 1))
    for e in range(1, 4):
        greet(section_of(z, flip(y, e // 2), flip(core, e % 2)), x)

    @pl.when(has_right)
    def _():
        greet(me + 4, x)

    @pl.when(has_left)
    def _():
        greet(me - 4, x)

    pl.semaphore_wait(barrier, 5 + jnp.where(has_right, 1, 0) + jnp.where(has_left, 1, 0))

    def exchange_copy(k, e, a):
        to_core = flip(core, e // 2)
        to_x = flip(x, e % 2)
        source = (q_hbm, g_hbm)[a]
        column = to_x * width + to_core * half_width + k * HD
        start = core * dec_count + x * rows
        args = (
            source.at[:, pl.ds(pl.multiple_of(column, HD), HD)],
            own.at[k, pl.ds(pl.multiple_of(start, rows), rows), a * HD : (a + 1) * HD],
        )
        if e == 0:
            return pltpu.make_async_copy(*args, a_recv.at[k, e, a])
        return pltpu.make_async_remote_copy(
            src_ref=args[0],
            dst_ref=args[1],
            send_sem=a_send.at[k, e, a],
            recv_sem=a_recv.at[k, e, a],
            device_id={"section": section_of(z, y, to_core), "tensor": to_x},
            device_id_type=MESH,
        )

    def exchange(k):
        for e in (3, 2, 1, 0):
            for a in range(2):
                exchange_copy(k, e, a).start()

    def memory_copy(k, ec):
        column = flip(core, ec) * half_width + k * HD
        ring = lax.rem(k, 2)
        return pltpu.make_async_copy(
            mem_hbm.at[:, :, pl.ds(pl.multiple_of(column, HD), HD)],
            mem_v.at[ring, :, :, ec * HD : (ec + 1) * HD],
            m_in.at[ring, ec],
        )

    def gradient_copy(k, ec):
        column = flip(core, ec) * half_width + k * HD
        ring = lax.rem(k, 2)
        return pltpu.make_async_copy(
            mg_v.at[ring, :, :, ec * HD : (ec + 1) * HD],
            mg_out.at[:, :, pl.ds(pl.multiple_of(column, HD), HD)],
            m_out.at[ring, ec],
        )

    def forward_copy(k, d):
        ring = lax.rem(k, RING)
        return pltpu.make_async_remote_copy(
            src_ref=out.at[ring, d],
            dst_ref=inc.at[k, d],
            send_sem=f_send.at[ring, d],
            recv_sem=f_recv.at[k, d],
            device_id={"section": me + (4, -4)[d]},
            device_id_type=MESH,
        )

    def return_copy(k, d):
        ring = lax.rem(k, RING)
        return pltpu.make_async_remote_copy(
            src_ref=rout.at[ring, d],
            dst_ref=rin.at[k, d],
            send_sem=r_send.at[ring, d],
            recv_sem=r_recv.at[k, d],
            device_id={"section": me + (-4, 4)[d]},
            device_id_type=MESH,
        )

    def slot_copy(send, recv, send_sem, recv_sem, k, e):
        ring = lax.rem(k, RING)
        if e == 0:
            return pltpu.make_async_copy(
                send.at[ring, :, e], recv.at[k, :, e], recv_sem.at[k, e]
            )
        return pltpu.make_async_remote_copy(
            src_ref=send.at[ring, :, e],
            dst_ref=recv.at[k, :, e],
            send_sem=send_sem.at[ring, e],
            recv_sem=recv_sem.at[k, e],
            device_id={"section": section_of(z, flip(y, e // 2), flip(core, e % 2))},
            device_id_type=MESH,
        )

    deliver_copy = functools.partial(slot_copy, dsend, drecv, d_send, d_recv)
    answer_copy = functools.partial(slot_copy, osend, oret, o_send, o_recv)

    def arrive(copy, e):
        if e == 0:
            copy.wait()
        else:
            copy.wait_recv()

    def last_copy(k, e, a):
        to_core = flip(core, e // 2)
        to_x = flip(x, e % 2)
        column = x * width + core * half_width + k * HD
        start = to_core * dec_count + to_x * rows
        args = (
            fin_v.at[k, pl.ds(pl.multiple_of(start, rows), rows), a * HD : (a + 1) * HD],
            (att_out, qg_out)[a].at[:, pl.ds(pl.multiple_of(column, HD), HD)],
        )
        if e == 0:
            return pltpu.make_async_copy(*args, g_recv.at[k, e, a])
        return pltpu.make_async_remote_copy(
            src_ref=args[0],
            dst_ref=args[1],
            send_sem=g_send.at[k, e, a],
            recv_sem=g_recv.at[k, e, a],
            device_id={"section": section_of(z, y, to_core), "tensor": to_x},
            device_id_type=MESH,
        )

    def last_arrival(k, e, a):
        from_core = flip(core, e // 2)
        from_x = flip(x, e % 2)
        column = from_x * width + from_core * half_width + k * HD
        start = core * dec_count + x * rows
        return pltpu.make_async_remote_copy(
            src_ref=fin_v.at[
                k, pl.ds(pl.multiple_of(start, rows), rows), a * HD : (a + 1) * HD
            ],
            dst_ref=(att_out, qg_out)[a].at[:, pl.ds(pl.multiple_of(column, HD), HD)],
            send_sem=g_send.at[k, e, a],
            recv_sem=g_recv.at[k, e, a],
            device_id={"section": section_of(z, y, from_core), "tensor": from_x},
            device_id_type=MESH,
        )

    for k in range(2):
        exchange(k)
    for copy in scalar_copies:
        copy.wait()

    for n in range(2 * ZS):
        source = section_of(n // 2, y, n % 2)
        start = jnp.int32(0)
        for i in range(PARTNERS):
            pre[n, i] = start
            start = start + dec_len[i, source]
        pre[n, PARTNERS] = start

    OUT_LEN, OUT_AT, OUT_FROM, IN_LEN, IN_AT, IN_FROM = range(6)
    for d in range(2):
        out_at, in_at = jnp.int32(0), jnp.int32(0)
        for n in range(2 * ZS):
            zs = n // 2
            if d == 0:
                begin = pre[n, 2 * z + 2]
                out_len = jnp.where(zs <= z, dec_count - begin, 0)
                first = pre[n, 2 * z]
                in_len = jnp.where(zs < z, dec_count - first, 0)
            else:
                begin, first = jnp.int32(0), jnp.int32(0)
                out_len = jnp.where(zs >= z, pre[n, 2 * z], 0)
                in_len = jnp.where(zs > z, pre[n, 2 * z + 2], 0)
            for name, value in (
                (OUT_LEN, out_len),
                (OUT_AT, out_at),
                (OUT_FROM, begin),
                (IN_LEN, in_len),
                (IN_AT, in_at),
                (IN_FROM, first),
            ):
                seg[d * 6 + name, n] = value
            out_at, in_at = out_at + out_len, in_at + in_len

    def part(d, name, n):
        return seg[d * 6 + name, n]

    def goal_of(count, pieces):
        position = iota((count, 1), 0)
        goal = jnp.full((count, 1), -1, jnp.int32)
        for at, length, column in pieces:
            within = position - at
            goal = jnp.where((within >= 0) & (within < length), within + column, goal)
        return goal

    for d in range(2):
        pieces = []
        for n in range(2 * ZS):
            zs, s = n // 2, n % 2
            column = jnp.where(
                zs == z,
                cap + s * dec_count + part(d, OUT_FROM, n),
                part(d, IN_AT, n) + part(d, OUT_FROM, n) - part(d, IN_FROM, n),
            )
            pieces.append((part(d, OUT_AT, n), part(d, OUT_LEN, n), column))
        fwd_m[d] = one_hot(iota((cap, cap + 2 * dec_count), 1) == goal_of(cap, pieces))

    @pl.when(~has_left)
    def _():
        inc[:, 0] = jnp.zeros(inc.shape[:1] + inc.shape[2:], BF16)
        rin[:, 1] = jnp.zeros(rin.shape[:1] + rin.shape[2:], BF16)

    @pl.when(~has_right)
    def _():
        inc[:, 1] = jnp.zeros(inc.shape[:1] + inc.shape[2:], BF16)
        rin[:, 0] = jnp.zeros(rin.shape[:1] + rin.shape[2:], BF16)

    def build_slots():
        for e in range(4):
            yy, s = flip(y, e // 2), 1 - flip(core, e % 2)
            i = 2 * z + yy
            at = slice(e * DEC_MAX, (e + 1) * DEC_MAX)
            for j in range(ZS - 1):
                zs = j + jnp.where(j >= z, 1, 0)
                n = zs * 2 + s
                d6 = jnp.where(zs < z, 0, 6)
                column = seg[d6 + IN_AT, n] + pre[n, i] - seg[d6 + IN_FROM, n]
                within = iota((DEC_MAX, cap), 0)
                hits = iota((DEC_MAX, cap), 1) - within == column
                hits = hits & (within < pre[n, i + 1] - pre[n, i])
                slot_m[j, at] = one_hot(hits)
            n = z * 2 + s
            column = s * dec_count + pre[n, i]
            within = iota((DEC_MAX, 2 * dec_count), 0)
            hits = iota((DEC_MAX, 2 * dec_count), 1) - within == column
            hits = hits & (within < pre[n, i + 1] - pre[n, i])
            ownslot_m[at] = one_hot(hits)

    def build_examples():
        for t in range(PARTNERS):
            ey, j = t // ZS, t % ZS
            zs = z if j == ZS - 1 else j + jnp.where(j >= z, 1, 0)
            reader = section_of(zs, flip(y, ey), 1 - core)
            start, begin, size = jnp.int32(0), jnp.int32(0), jnp.int32(0)
            for i in range(PARTNERS):
                length = enc_len[i, me]
                match = readers[i, me] == reader
                begin = jnp.where(match, start, begin)
                size = jnp.where(match, length, size)
                start = start + length
            meta[0, t] = begin
            meta[1, t] = size
        mem_f[:, :, enc_count:] = jnp.zeros((2, 2, ENC_MAX, HD), F32)
        pieces = [(meta[0, t], meta[1, t], t * ENC_MAX) for t in range(PARTNERS)]
        goal = goal_of(enc_count, pieces)
        for b in range(enc_count // 256):
            at = slice(b * 256, (b + 1) * 256)
            grad_m[at, :] = one_hot(iota((256, PARTNERS * ENC_MAX), 1) == goal[at])

    remote = (ZS - 1) * 4 * DEC_MAX

    def build_returns():
        for d in range(2):
            pieces = []
            for n in range(2 * ZS):
                zs, s = n // 2, n % 2
                valid = part(d, IN_LEN, n) > 0
                shift = part(d, IN_AT, n) - part(d, IN_FROM, n)
                j = zs - jnp.where(zs > z, 1, 0)
                ec = lax.rem(1 - s - core + 2, 2)
                for yy in range(2):
                    e = lax.rem(yy - y + 2, 2) * 2 + ec
                    begin = pre[n, 2 * z + yy]
                    length = jnp.where(valid, pre[n, 2 * z + yy + 1] - begin, 0)
                    pieces.append((shift + begin, length, (j * 4 + e) * DEC_MAX))
                begin = pre[n, 2 * z + 2] if d == 0 else jnp.int32(0)
                length = dec_count - begin if d == 0 else pre[n, 2 * z]
                column = remote + part(d, OUT_AT, n)
                pieces.append((shift + begin, jnp.where(valid, length, 0), column))
            ret_m[d] = one_hot(iota((cap, remote + cap), 1) == goal_of(cap, pieces))

        pieces = []
        local = 4 * DEC_MAX
        for s in range(2):
            n = z * 2 + s
            ec = lax.rem(1 - s - core + 2, 2)
            for yy in range(2):
                e = lax.rem(yy - y + 2, 2) * 2 + ec
                begin = pre[n, 2 * z + yy]
                length = pre[n, 2 * z + yy + 1] - begin
                pieces.append((s * dec_count + begin, length, e * DEC_MAX))
            begin = pre[n, 2 * z + 2]
            at = s * dec_count
            pieces.append((at + begin, dec_count - begin, local + seg[OUT_AT, n]))
            pieces.append((at, pre[n, 2 * z], local + cap + seg[6 + OUT_AT, n]))
        count = 2 * dec_count
        fin_m[...] = one_hot(iota((count, local + 2 * cap), 1) == goal_of(count, pieces))

    def forward(k, d, starts):
        ring = lax.rem(k, RING)

        @pl.when(k >= RING)
        def _():
            forward_copy(k - RING, d).wait_send()

        @pl.when(jnp.logical_not(starts))
        def _():
            forward_copy(k, d).wait_recv()
            block = matmul(fwd_m[d, :, :cap], inc[k, d], NN)
            block = block + matmul(fwd_m[d, :, cap:], own[k], NN)
            out[ring, d] = block.astype(BF16)

        @pl.when(starts)
        def _():
            out[ring, d] = matmul(fwd_m[d, :, cap:], own[k], NN).astype(BF16)

        forward_copy(k, d).start()

    def deliver(k):
        ring = lax.rem(k, RING)

        @pl.when(z == ZS - 1)
        def _():
            forward_copy(k, 0).wait_recv()

        @pl.when(z == 0)
        def _():
            forward_copy(k, 1).wait_recv()

        @pl.when(k >= RING)
        def _():
            for e in range(1, 4):
                deliver_copy(k - RING, e).wait_send()

        for j in range(ZS - 1):
            d = jnp.where(j < z, 0, 1)
            block = matmul(slot_m[j], inc[k, d], NN).astype(BF16)
            dsend[ring, j] = block.reshape(4, DEC_MAX, 2 * HD)
        block = matmul(ownslot_m[...], own[k], NN).astype(BF16)
        dsend[ring, ZS - 1] = block.reshape(4, DEC_MAX, 2 * HD)
        for e in (3, 2, 1, 0):
            deliver_copy(k, e).start()

    def attend(k):
        ring = lax.rem(k, RING)
        pair = lax.rem(k, 2)
        for ec in range(2):
            memory_copy(k, ec).wait()
        for a in range(2):
            for ec in range(2):
                at = slice(ec * HD, (ec + 1) * HD)
                mem_f[a, ec, :enc_count] = mem_v[pair, a, :, at].astype(F32)

        @pl.when(k + 2 < chunks)
        def _():
            for ec in range(2):
                memory_copy(k + 2, ec).start()

        @pl.when(k >= RING)
        def _():
            for e in range(1, 4):
                answer_copy(k - RING, e).wait_send()

        for e in range(4):
            arrive(deliver_copy(k, e), e)

        @pl.loop(0, 2)
        def _(ey):
            units = [(ey * ZS + j, j, ec) for j in range(ZS) for ec in range(2)]
            column = iota((DEC_MAX, ENC_MAX), 1)

            def tokens(unit, a):
                t, j, ec = unit
                return drecv[k, j, ey * 2 + ec, :, a * HD : (a + 1) * HD]

            def example(unit, a):
                t, j, ec = unit
                return mem_f[a, ec, pl.ds(meta[0, t], ENC_MAX)].astype(BF16)

            keys = [example(unit, 0) for unit in units]
            values = [example(unit, 1) for unit in units]
            scores = [matmul(tokens(u, 0), key, NT) for u, key in zip(units, keys)]
            dprobs = [matmul(tokens(u, 1), value, NT) for u, value in zip(units, values)]
            scores = [jnp.where(column < meta[1, u[0]], s, -jnp.inf) for u, s in zip(units, scores)]
            most = [jnp.max(s, axis=1, keepdims=True) for s in scores]
            weights = [jnp.exp((s - m) * scaling) for s, m in zip(scores, most)]
            scale = [1.0 / jnp.sum(w, axis=1, keepdims=True) for w in weights]
            probs = [w * r for w, r in zip(weights, scale)]
            delta = [jnp.sum(w * d, axis=1, keepdims=True) for w, d in zip(probs, dprobs)]
            low = [w.astype(BF16) for w in probs]
            dscores = [
                (w * (d - e)).astype(BF16) for w, d, e in zip(probs, dprobs, delta)
            ]
            for i, (t, j, ec) in enumerate(units):
                e = ey * 2 + ec
                at = slice(ec * HD, (ec + 1) * HD)
                osend[ring, j, e, :, :HD] = matmul(low[i], values[i], NN).astype(BF16)
                block = matmul(dscores[i], keys[i], NN) * scaling
                osend[ring, j, e, :, HD:] = block.astype(BF16)
                block = matmul(dscores[i], tokens(units[i], 0), TN) * scaling
                d_x[0, t, :, at] = block.astype(BF16)
                d_x[1, t, :, at] = matmul(low[i], tokens(units[i], 1), TN).astype(BF16)

        for e in (3, 2, 1, 0):
            answer_copy(k, e).start()

    def collect(k):
        pair = lax.rem(k, 2)

        @pl.when(k >= 2)
        def _():
            for ec in range(2):
                gradient_copy(k - 2, ec).wait()

        for a in range(2):

            @pl.loop(0, enc_count // 256)
            def _(b):
                at = pl.ds(pl.multiple_of(b * 256, 256), 256)
                block = d_x[a].reshape(PARTNERS * ENC_MAX, 2 * HD)
                mg_v[pair, a, at] = matmul(grad_m[at, :], block, NN).astype(BF16)

        for ec in range(2):
            gradient_copy(k, ec).start()

    def answers(k):
        for e in range(4):
            arrive(answer_copy(k, e), e)

    def give_back(k, d, starts):
        ring = lax.rem(k, RING)

        @pl.when(k >= RING)
        def _():
            return_copy(k - RING, d).wait_send()

        answered = oret[k, : ZS - 1].reshape(remote, 2 * HD)

        @pl.when(jnp.logical_not(starts))
        def _():
            return_copy(k, d).wait_recv()
            block = matmul(ret_m[d, :, :remote], answered, NN)
            block = block + matmul(ret_m[d, :, remote:], rin[k, d], NN)
            rout[ring, d] = block.astype(BF16)

        @pl.when(starts)
        def _():
            rout[ring, d] = matmul(ret_m[d, :, :remote], answered, NN).astype(BF16)

        return_copy(k, d).start()

    def finish(k):
        @pl.when(z == 0)
        def _():
            return_copy(k, 0).wait_recv()

        @pl.when(z == ZS - 1)
        def _():
            return_copy(k, 1).wait_recv()

        local = 4 * DEC_MAX
        block = matmul(fin_m[:, :local], oret[k, ZS - 1].reshape(local, 2 * HD), NN)
        for d in range(2):
            at = local + d * cap
            block = block + matmul(fin_m[:, at : at + cap], rin[k, d], NN)
        fin_v[k] = block.astype(BF16)
        for e in (3, 2, 1, 0):
            for a in range(2):
                last_copy(k, e, a).start()

    for k in range(2):
        for ec in range(2):
            memory_copy(k, ec).start()

    near = ZS - 1
    lag = 2
    back = lag * near + 2
    settled = lag * far + jnp.where(far < near, 3, 2)
    steps = chunks + back + lag * near

    def during(k, condition=None):
        go = (k >= 0) & (k < chunks)
        if condition is not None:
            go = go & condition
        return pl.when(go)

    @pl.loop(0, steps)
    def _(t):
        @during(t)
        def _():
            for e in range(4):
                for a in range(2):
                    arrive(exchange_copy(t, e, a), e)

            @pl.when(t + 2 < chunks)
            def _():
                exchange(t + 2)

        @during(t - lag * z, has_right)
        def _():
            forward(t - lag * z, 0, z == 0)

        @during(t - lag * (near - z), has_left)
        def _():
            forward(t - lag * (near - z), 1, z == near)

        @pl.when(t == 0)
        def _():
            build_slots()
            build_examples()
            build_returns()

        @during(t - settled)
        def _():
            answers(t - settled)

        @during(t - back - lag * (near - z), has_left)
        def _():
            give_back(t - back - lag * (near - z), 0, z == near)

        @during(t - back - lag * z, has_right)
        def _():
            give_back(t - back - lag * z, 1, z == 0)

        @during(t - lag * far)
        def _():
            deliver(t - lag * far)

        @during(t - lag * far - 1)
        def _():
            attend(t - lag * far - 1)

        @during(t - lag * far - 1)
        def _():
            collect(t - lag * far - 1)

        @during(t - back - lag * far)
        def _():
            finish(t - back - lag * far)

    @pl.loop(0, chunks)
    def _(k):
        for e in range(4):
            for a in range(2):
                if e == 0:
                    last_copy(k, e, a).wait()
                else:
                    exchange_copy(k, e, a).wait_send()
                    last_copy(k, e, a).wait_send()
                    last_arrival(k, e, a).wait_recv()

    @pl.loop(chunks - RING, chunks)
    def _(k):
        for e in range(1, 4):
            deliver_copy(k, e).wait_send()
            answer_copy(k, e).wait_send()

        @pl.when(has_right)
        def _():
            forward_copy(k, 0).wait_send()
            return_copy(k, 1).wait_send()

        @pl.when(has_left)
        def _():
            forward_copy(k, 1).wait_send()
            return_copy(k, 0).wait_send()

    @pl.loop(chunks - 2, chunks)
    def _(k):
        for ec in range(2):
            gradient_copy(k, ec).wait()


def packed_body(memory, queries, out_grad, enc_lengths, dec_lengths, readers):
    enc_count, width = memory.shape[1:]
    rows = queries.shape[0]
    count = 4 * rows
    chunks = width // 2 // HD
    pair = 2 * HD
    scalars = (enc_lengths.T, dec_lengths.T, readers.T)
    anywhere = pl.BlockSpec(memory_space=pl.ANY)
    dma = pltpu.SemaphoreType.DMA
    blocks = (ZS, 4, DEC_MAX, pair)
    local = 4 * DEC_MAX
    remote = (ZS - 1) * local

    def vmem(*shape):
        return pltpu.VMEM(shape, BF16)

    return pl.pallas_call(
        packed_kernel,
        out_shape=(
            jax.ShapeDtypeStruct(queries.shape, BF16),
            jax.ShapeDtypeStruct(queries.shape, BF16),
            jax.ShapeDtypeStruct(memory.shape, BF16),
        ),
        in_specs=[anywhere] * 6,
        out_specs=(anywhere,) * 3,
        scratch_shapes=[
            vmem(chunks, count, pair),
            vmem(chunks, 2, CAP, pair),
            vmem(RING, 2, CAP, pair),
            vmem(RING, *blocks),
            vmem(chunks, *blocks),
            vmem(RING, *blocks),
            vmem(chunks, *blocks),
            vmem(chunks, 2, CAP, pair),
            vmem(RING, 2, CAP, pair),
            vmem(chunks, count, pair),
            vmem(2, 2, enc_count, pair),
            vmem(2, 2, enc_count, pair),
            pltpu.VMEM((2, 2, enc_count + ENC_MAX, HD), F32),
            vmem(2, PARTNERS, ENC_MAX, pair),
            vmem(2, CAP, CAP + count),
            vmem(ZS - 1, local, CAP),
            vmem(local, count),
            vmem(2, CAP, remote + CAP),
            vmem(count, local + 2 * CAP),
            vmem(enc_count, PARTNERS * ENC_MAX),
            *[pltpu.SMEM(array.shape, jnp.int32) for array in scalars],
            pltpu.SMEM((2 * ZS, PARTNERS + 1), jnp.int32),
            pltpu.SMEM((12, 2 * ZS), jnp.int32),
            pltpu.SMEM((2, PARTNERS), jnp.int32),
            dma((chunks, 4, 2)),
            dma((chunks, 4, 2)),
            dma((RING, 2)),
            dma((chunks, 2)),
            dma((RING, 4)),
            dma((chunks, 4)),
            dma((RING, 4)),
            dma((chunks, 4)),
            dma((RING, 2)),
            dma((chunks, 2)),
            dma((chunks, 4, 2)),
            dma((chunks, 4, 2)),
            dma((2, 2)),
            dma((2, 2)),
            dma((3,)),
        ],
        compiler_params=pltpu.CompilerParams(
            collective_id=1, has_side_effects=True, vmem_limit_bytes=60 * 1024 * 1024
        ),
    )(memory, queries, out_grad, *scalars)


def most_rows(dec_lengths):
    place = np.arange(2 * ZS * 2 * 2 * ZS).reshape(4 * ZS, 2 * ZS)
    source, half = place // (8 * ZS), place // (4 * ZS) % 2
    goal = place % (2 * ZS) // 2
    blocks = []
    for cut in range(1, ZS):
        for y in range(2):
            blocks.append((half == y) & (source < cut) & (goal >= cut))
            blocks.append((half == y) & (source >= cut) & (goal < cut))
    counts = jnp.where(np.stack(blocks), dec_lengths, 0)
    return jnp.max(jnp.sum(counts, axis=(1, 2)))


def body(sections, tensors, *args):
    packs = (sections, tensors) == (4 * ZS, 2)
    padded = functools.partial(padded_body, sections, tensors, packs)
    if not packs:
        return padded(*args)
    return lax.cond(most_rows(args[4]) <= CAP, packed_body, padded, *args)


def solution(mesh):
    placed = (
        P(None, "section", "tensor"),
        P(("section", "tensor"), None),
        P(("section", "tensor"), None),
        P(),
        P(),
        P(),
    )
    return jax.shard_map(
        functools.partial(body, mesh.shape["section"], mesh.shape["tensor"]),
        mesh=mesh,
        in_specs=placed,
        out_specs=(
            P(("section", "tensor"), None),
            P(("section", "tensor"), None),
            P(None, "section", "tensor"),
        ),
        check_vma=False,
    )
```

```python
import functools

import jax
import jax.numpy as jnp
import numpy as np
from jax import lax
from jax.experimental import pallas as pl
from jax.experimental.pallas import tpu as pltpu
from jax.sharding import PartitionSpec as P

HD = 128
ENC_MAX = 128
DEC_MAX = 64
PARTNERS = 8
MOST_CHUNKS = 8
BF16 = jnp.bfloat16
F32 = jnp.float32
MESH = pl.DeviceIdType.MESH


def matmul(a, b, dims):
    return lax.dot_general(a, b, (dims, ((), ())), preferred_element_type=F32)


NN = ((1,), (0,))
NT = ((1,), (1,))
TN = ((0,), (0,))


def chunk_count(width):
    return min(MOST_CHUNKS, width // HD)


def staged_kernel(sections, tensors, *refs):
    inputs, results, staging = refs[:6], refs[6:9], refs[9:12]
    sem = refs[-1]
    kernel(sections, tensors, *inputs, *staging, *refs[12:-1])
    copies = [
        pltpu.make_async_copy(source, target, sem.at[i])
        for i, (source, target) in enumerate(zip(staging, results))
    ]
    for copy in copies:
        copy.start()
    for copy in copies:
        copy.wait()


def kernel(
    sections,
    tensors,
    mem_hbm,
    q_hbm,
    g_hbm,
    enc_hbm,
    dec_hbm,
    readers_hbm,
    att_out,
    qg_out,
    mg_out,
    mem_v,
    dec_v,
    fsend,
    frecv,
    osend,
    oret,
    fin_v,
    kv_x,
    d_x,
    pack_m,
    unpack_m,
    enc_m,
    grad_m,
    enc_len,
    dec_len,
    readers,
    meta,
    a_send,
    a_recv,
    a_local,
    f_send,
    f_recv,
    o_send,
    o_recv,
    g_send,
    g_recv,
    g_local,
    m_in,
    s_in,
):
    me = lax.axis_index("section")
    mine = lax.axis_index("tensor")
    rows = q_hbm.shape[0]
    enc_count = mem_v.shape[1]
    dec_count = dec_v.shape[2]
    width = mem_v.shape[2]
    chunks = chunk_count(width)
    piece = width // chunks
    spacing = sections // PARTNERS
    scaling = HD ** (-0.5)

    def holder_of(slot):
        return lax.rem(me + 2 * sections - slot * spacing - 1, sections)

    def reader_of(slot):
        return lax.rem(me + slot * spacing + 1, sections)

    half = PARTNERS // 2

    def peer_of(step):
        return lax.rem(mine + step, tensors)

    mem_copy = pltpu.make_async_copy(mem_hbm, mem_v, m_in)
    scalar_copies = [
        pltpu.make_async_copy(source, target, s_in.at[i])
        for i, (source, target) in enumerate(
            ((enc_hbm, enc_len), (dec_hbm, dec_len), (readers_hbm, readers))
        )
    ]
    for copy in scalar_copies:
        copy.start()

    barrier = pltpu.get_barrier_semaphore()
    for step in range(1, tensors):
        pl.semaphore_signal(
            barrier, inc=1, device_id={"tensor": peer_of(step)}, device_id_type=MESH
        )
    for slot in range(PARTNERS):
        pl.semaphore_signal(
            barrier, inc=1, device_id={"section": holder_of(slot)}, device_id_type=MESH
        )
        pl.semaphore_signal(
            barrier, inc=1, device_id={"section": reader_of(slot)}, device_id_type=MESH
        )
    pl.semaphore_wait(barrier, tensors - 1 + 2 * PARTNERS)

    own_rows = pl.ds(pl.multiple_of(mine * rows, rows), rows)

    def first_copy(c, a, step):
        peer = peer_of(step)
        source = (q_hbm, g_hbm)[a]
        columns = pl.ds(pl.multiple_of(peer * width + c * piece, piece), piece)
        if step == 0:
            return pltpu.make_async_copy(
                source.at[:, columns], dec_v.at[c, a, own_rows], a_local.at[c, a]
            )
        return pltpu.make_async_remote_copy(
            src_ref=source.at[:, columns],
            dst_ref=dec_v.at[c, a, own_rows],
            send_sem=a_send.at[c, a, step - 1],
            recv_sem=a_recv.at[c, a, step - 1],
            device_id={"tensor": peer},
            device_id_type=MESH,
        )

    def fetch(c):
        for a in range(2):
            for step in list(range(1, tensors)) + [0]:
                first_copy(c, a, step).start()

    fetch(0)
    mem_copy.start()
    for copy in scalar_copies:
        copy.wait()

    start = jnp.int32(0)
    for i in range(PARTNERS):
        length = dec_len[i, me]
        meta[0, i] = start
        meta[1, i] = length
        start = start + length
    for slot in range(PARTNERS):
        reader = reader_of(slot)
        start, begin, size = jnp.int32(0), jnp.int32(0), jnp.int32(0)
        for j in range(PARTNERS):
            length = enc_len[j, me]
            match = readers[j, me] == reader
            begin = jnp.where(match, start, begin)
            size = jnp.where(match, length, size)
            start = start + length
        meta[2, slot] = begin
        meta[3, slot] = size

    def one_hot(hits):
        return jnp.where(hits, 1.0, 0.0).astype(BF16)

    def iota(shape, dim):
        return lax.broadcasted_iota(jnp.int32, shape, dim)

    for i in range(PARTNERS):
        shape = (DEC_MAX, dec_count)
        within = iota(shape, 0)
        hits = (iota(shape, 1) - within == meta[0, i]) & (within < meta[1, i])
        pack_m[i // half, (i % half) * DEC_MAX : (i % half + 1) * DEC_MAX, :] = one_hot(hits)

    def forward_copy(c, slot):
        holder = holder_of(slot)
        return pltpu.make_async_remote_copy(
            src_ref=fsend.at[c, :, lax.div(holder, spacing)],
            dst_ref=frecv.at[c, :, slot],
            send_sem=f_send.at[c, slot],
            recv_sem=f_recv.at[c, slot],
            device_id={"section": holder},
            device_id_type=MESH,
        )

    def back_copy(c, slot):
        return pltpu.make_async_remote_copy(
            src_ref=osend.at[c, :, slot],
            dst_ref=oret.at[c, :, lax.div(me, spacing)],
            send_sem=o_send.at[c, slot],
            recv_sem=o_recv.at[c, lax.div(me, spacing)],
            device_id={"section": reader_of(slot)},
            device_id_type=MESH,
        )

    def back_arrival(c, i):
        return pltpu.make_async_remote_copy(
            src_ref=osend.at[c, :, i],
            dst_ref=oret.at[c, :, i],
            send_sem=o_send.at[c, i],
            recv_sem=o_recv.at[c, i],
            device_id={"section": reader_of(i)},
            device_id_type=MESH,
        )

    def last_copy(c, a, step):
        peer = peer_of(step)
        target = (att_out, qg_out)[a]
        source = fin_v.at[c, a, pl.ds(pl.multiple_of(peer * rows, rows), rows)]
        columns = pl.ds(pl.multiple_of(mine * width + c * piece, piece), piece)
        if step == 0:
            return pltpu.make_async_copy(source, target.at[:, columns], g_local.at[c, a])
        return pltpu.make_async_remote_copy(
            src_ref=source,
            dst_ref=target.at[:, columns],
            send_sem=g_send.at[c, a, step - 1],
            recv_sem=g_recv.at[c, a, step - 1],
            device_id={"tensor": peer},
            device_id_type=MESH,
        )

    def pack(c):
        for a in range(2):
            first_copy(c, a, 0).wait()
            for step in range(1, tensors):
                first_copy(c, a, step).wait_recv()
        if c + 1 < chunks:
            fetch(c + 1)
        for a in range(2):
            for g in range(2):
                block = matmul(pack_m[g], dec_v[c, a], NN).astype(BF16)
                fsend[c, a, g * half : (g + 1) * half] = block.reshape(half, DEC_MAX, piece)

        @pl.loop(0, PARTNERS)
        def _(turn):
            forward_copy(c, turn).start()

    def expand(c):
        @pl.loop(0, PARTNERS // 2)
        def _(g):
            for a in range(2):
                block = matmul(enc_m[g], mem_v[a, :, c * piece : (c + 1) * piece], NN)
                kv_x[c, a, pl.ds(g * 2, 2)] = block.astype(BF16).reshape(2, ENC_MAX, piece)

    def attend(c):
        @pl.loop(0, PARTNERS)
        def _(turn):
            slot = turn
            forward_copy(c, slot).wait_recv()
            valid = iota((DEC_MAX, ENC_MAX), 1) < meta[3, slot]
            for h in range(piece // HD):
                at = slice(h * HD, (h + 1) * HD)
                q = frecv[c, 0, slot, :, at]
                g = frecv[c, 1, slot, :, at]
                k = kv_x[c, 0, slot, :, at]
                v = kv_x[c, 1, slot, :, at]
                scores = jnp.where(valid, matmul(q, k, NT) * scaling, -jnp.inf)
                weights = jnp.exp(scores - jnp.max(scores, axis=1, keepdims=True))
                probs = weights / jnp.sum(weights, axis=1, keepdims=True)
                low = probs.astype(BF16)
                dprobs = matmul(g, v, NT)
                delta = jnp.sum(probs * dprobs, axis=1, keepdims=True)
                dscores = (probs * (dprobs - delta)).astype(BF16)
                osend[c, 0, slot, :, at] = matmul(low, v, NN).astype(BF16)
                osend[c, 1, slot, :, at] = (matmul(dscores, k, NN) * scaling).astype(BF16)
                d_x[0, slot, :, at] = (matmul(dscores, q, TN) * scaling).astype(BF16)
                d_x[1, slot, :, at] = matmul(low, g, TN).astype(BF16)
            back_copy(c, slot).start()

    def collect(c):
        @pl.loop(0, enc_count // 256)
        def _(b):
            at = pl.ds(pl.multiple_of(b * 256, 256), 256)
            for a in range(2):
                block = d_x[a].reshape(PARTNERS * ENC_MAX, piece)
                mg_out[a, at, c * piece : (c + 1) * piece] = matmul(
                    grad_m[at, :], block, NN
                ).astype(BF16)

    def finish(c):
        @pl.loop(0, PARTNERS)
        def _(i):
            back_arrival(c, i).wait_recv()

        for a in range(2):
            block = oret[c, a].reshape(PARTNERS * DEC_MAX, piece)
            fin_v[c, a] = matmul(unpack_m[...], block, NN).astype(BF16)
            for step in list(range(1, tensors)) + [0]:
                last_copy(c, a, step).start()

    def settle():
        for c in range(chunks):
            for a in range(2):
                for step in range(1, tensors):
                    first_copy(c, a, step).wait_send()

            @pl.loop(0, PARTNERS)
            def _(slot):
                forward_copy(c, slot).wait_send()
                back_copy(c, slot).wait_send()

    pack(0)

    for slot in range(PARTNERS):
        shape = (ENC_MAX, enc_count)
        within = iota(shape, 0)
        hits = (iota(shape, 1) - within == meta[2, slot]) & (within < meta[3, slot])
        enc_m[slot // 2, (slot % 2) * ENC_MAX : (slot % 2 + 1) * ENC_MAX, :] = one_hot(hits)
    mem_copy.wait()
    expand(0)
    pack(1)

    position = iota((dec_count, 1), 0)
    goal = jnp.full((dec_count, 1), -1, jnp.int32)
    for i in range(PARTNERS):
        within = position - meta[0, i]
        goal = jnp.where((within >= 0) & (within < meta[1, i]), within + i * DEC_MAX, goal)
    unpack_m[...] = one_hot(iota((dec_count, PARTNERS * DEC_MAX), 1) == goal)
    for b in range(enc_count // 256):
        position = iota((256, 1), 0) + b * 256
        goal = jnp.full((256, 1), -1, jnp.int32)
        for slot in range(PARTNERS):
            within = position - meta[2, slot]
            goal = jnp.where(
                (within >= 0) & (within < meta[3, slot]), within + slot * ENC_MAX, goal
            )
        hits = iota((256, PARTNERS * ENC_MAX), 1) == goal
        grad_m[b * 256 : (b + 1) * 256, :] = one_hot(hits)

    expand(1)
    for c in range(2, chunks):
        pack(c)
        expand(c)
    for c in range(chunks):
        attend(c)
        collect(c)
        if c >= 3:
            finish(c - 3)
    for c in range(max(chunks - 3, 0), chunks):
        if c == chunks - 1:
            settle()
        finish(c)

    for c in range(chunks):
        for a in range(2):
            for step in range(1, tensors):
                last_copy(c, a, step).wait()
            last_copy(c, a, 0).wait()


def padded_body(sections, tensors, staged, memory, queries, out_grad, enc_lengths, dec_lengths, readers):
    enc_count, width = memory.shape[1:]
    rows = queries.shape[0]
    dec_count = rows * tensors
    chunks = chunk_count(width)
    piece = width // chunks
    blocks = (chunks, 2, PARTNERS, DEC_MAX, piece)
    peers = max(tensors - 1, 1)
    scalars = (enc_lengths.T, dec_lengths.T, readers.T)
    anywhere = pl.BlockSpec(memory_space=pl.ANY)
    resident = pl.BlockSpec(memory_space=pltpu.VMEM)
    results = [array.shape for array in (queries, queries, memory)]
    dma = pltpu.SemaphoreType.DMA
    return pl.pallas_call(
        functools.partial(staged_kernel if staged else kernel, sections, tensors),
        out_shape=tuple(
            jax.ShapeDtypeStruct(shape, BF16) if staged else pltpu.VMEM(shape, BF16)
            for shape in results
        ),
        in_specs=[anywhere] * 6,
        out_specs=(anywhere if staged else resident,) * 3,
        scratch_shapes=[
            *[pltpu.VMEM(shape, BF16) for shape in results if staged],
            pltpu.VMEM((2, enc_count, width), BF16),
            pltpu.VMEM((chunks, 2, dec_count, piece), BF16),
            pltpu.VMEM(blocks, BF16),
            pltpu.VMEM(blocks, BF16),
            pltpu.VMEM(blocks, BF16),
            pltpu.VMEM(blocks, BF16),
            pltpu.VMEM((chunks, 2, dec_count, piece), BF16),
            pltpu.VMEM((chunks, 2, PARTNERS, ENC_MAX, piece), BF16),
            pltpu.VMEM((2, PARTNERS, ENC_MAX, piece), BF16),
            pltpu.VMEM((2, PARTNERS // 2 * DEC_MAX, dec_count), BF16),
            pltpu.VMEM((dec_count, PARTNERS * DEC_MAX), BF16),
            pltpu.VMEM((PARTNERS // 2, 2 * ENC_MAX, enc_count), BF16),
            pltpu.VMEM((enc_count, PARTNERS * ENC_MAX), BF16),
            *[pltpu.SMEM(array.shape, jnp.int32) for array in scalars],
            pltpu.SMEM((4, PARTNERS), jnp.int32),
            dma((chunks, 2, peers)),
            dma((chunks, 2, peers)),
            dma((chunks, 2)),
            dma((chunks, PARTNERS)),
            dma((chunks, PARTNERS)),
            dma((chunks, PARTNERS)),
            dma((chunks, PARTNERS)),
            dma((chunks, 2, peers)),
            dma((chunks, 2, peers)),
            dma((chunks, 2)),
            dma,
            dma((3,)),
            *[dma((3,))] * staged,
        ],
        compiler_params=pltpu.CompilerParams(
            collective_id=0, has_side_effects=True, vmem_limit_bytes=(56 if staged else 46) * 1024 * 1024
        ),
    )(memory, queries, out_grad, *scalars)


ZS = 4
CAP = 640
RING = 4


def packed_kernel(
    mem_hbm,
    q_hbm,
    g_hbm,
    enc_hbm,
    dec_hbm,
    readers_hbm,
    att_out,
    qg_out,
    mg_out,
    own,
    inc,
    out,
    dsend,
    drecv,
    osend,
    oret,
    rin,
    rout,
    fin_v,
    mem_v,
    mg_v,
    mem_f,
    d_x,
    fwd_m,
    slot_m,
    ownslot_m,
    ret_m,
    fin_m,
    grad_m,
    enc_len,
    dec_len,
    readers,
    pre,
    seg,
    meta,
    a_send,
    a_recv,
    f_send,
    f_recv,
    d_send,
    d_recv,
    o_send,
    o_recv,
    r_send,
    r_recv,
    g_send,
    g_recv,
    m_in,
    m_out,
    s_in,
):
    me = lax.axis_index("section")
    x = lax.axis_index("tensor")
    z = lax.div(me, 4)
    y = lax.rem(lax.div(me, 2), 2)
    core = lax.rem(me, 2)
    rows = q_hbm.shape[0]
    dec_count = 2 * rows
    enc_count = mem_hbm.shape[1]
    width = mem_hbm.shape[2]
    half_width = width // 2
    chunks = half_width // HD
    cap = inc.shape[2]
    scaling = HD ** (-0.5)
    has_right = z < ZS - 1
    has_left = z > 0
    far = jnp.maximum(z, ZS - 1 - z)

    def flip(value, step):
        return lax.rem(value + step, 2)

    def section_of(zz, yy, cc):
        return zz * 4 + yy * 2 + cc

    def iota(shape, dim):
        return lax.broadcasted_iota(jnp.int32, shape, dim)

    def one_hot(hits):
        return jnp.where(hits, 1.0, 0.0).astype(BF16)

    scalar_copies = [
        pltpu.make_async_copy(source, target, s_in.at[i])
        for i, (source, target) in enumerate(
            ((enc_hbm, enc_len), (dec_hbm, dec_len), (readers_hbm, readers))
        )
    ]
    for copy in scalar_copies:
        copy.start()

    barrier = pltpu.get_barrier_semaphore()

    def greet(section, tensor):
        pl.semaphore_signal(
            barrier,
            inc=1,
            device_id={"section": section, "tensor": tensor},
            device_id_type=MESH,
        )

    greet(section_of(z, y, core), flip(x, 1))
    greet(section_of(z, y, flip(core, 1)), flip(x, 1))
    for e in range(1, 4):
        greet(section_of(z, flip(y, e // 2), flip(core, e % 2)), x)

    @pl.when(has_right)
    def _():
        greet(me + 4, x)

    @pl.when(has_left)
    def _():
        greet(me - 4, x)

    pl.semaphore_wait(barrier, 5 + jnp.where(has_right, 1, 0) + jnp.where(has_left, 1, 0))

    def exchange_copy(k, e, a):
        to_core = flip(core, e // 2)
        to_x = flip(x, e % 2)
        source = (q_hbm, g_hbm)[a]
        column = to_x * width + to_core * half_width + k * HD
        start = core * dec_count + x * rows
        args = (
            source.at[:, pl.ds(pl.multiple_of(column, HD), HD)],
            own.at[k, pl.ds(pl.multiple_of(start, rows), rows), a * HD : (a + 1) * HD],
        )
        if e == 0:
            return pltpu.make_async_copy(*args, a_recv.at[k, e, a])
        return pltpu.make_async_remote_copy(
            src_ref=args[0],
            dst_ref=args[1],
            send_sem=a_send.at[k, e, a],
            recv_sem=a_recv.at[k, e, a],
            device_id={"section": section_of(z, y, to_core), "tensor": to_x},
            device_id_type=MESH,
        )

    def exchange(k):
        for e in (3, 2, 1, 0):
            for a in range(2):
                exchange_copy(k, e, a).start()

    def memory_copy(k, ec):
        column = flip(core, ec) * half_width + k * HD
        ring = lax.rem(k, 2)
        return pltpu.make_async_copy(
            mem_hbm.at[:, :, pl.ds(pl.multiple_of(column, HD), HD)],
            mem_v.at[ring, :, :, ec * HD : (ec + 1) * HD],
            m_in.at[ring, ec],
        )

    def gradient_copy(k, ec):
        column = flip(core, ec) * half_width + k * HD
        ring = lax.rem(k, 2)
        return pltpu.make_async_copy(
            mg_v.at[ring, :, :, ec * HD : (ec + 1) * HD],
            mg_out.at[:, :, pl.ds(pl.multiple_of(column, HD), HD)],
            m_out.at[ring, ec],
        )

    def forward_copy(k, d):
        ring = lax.rem(k, RING)
        return pltpu.make_async_remote_copy(
            src_ref=out.at[ring, d],
            dst_ref=inc.at[k, d],
            send_sem=f_send.at[ring, d],
            recv_sem=f_recv.at[k, d],
            device_id={"section": me + (4, -4)[d]},
            device_id_type=MESH,
        )

    def return_copy(k, d):
        ring = lax.rem(k, RING)
        return pltpu.make_async_remote_copy(
            src_ref=rout.at[ring, d],
            dst_ref=rin.at[k, d],
            send_sem=r_send.at[ring, d],
            recv_sem=r_recv.at[k, d],
            device_id={"section": me + (-4, 4)[d]},
            device_id_type=MESH,
        )

    def slot_copy(send, recv, send_sem, recv_sem, k, e):
        ring = lax.rem(k, RING)
        if e == 0:
            return pltpu.make_async_copy(
                send.at[ring, :, e], recv.at[k, :, e], recv_sem.at[k, e]
            )
        return pltpu.make_async_remote_copy(
            src_ref=send.at[ring, :, e],
            dst_ref=recv.at[k, :, e],
            send_sem=send_sem.at[ring, e],
            recv_sem=recv_sem.at[k, e],
            device_id={"section": section_of(z, flip(y, e // 2), flip(core, e % 2))},
            device_id_type=MESH,
        )

    deliver_copy = functools.partial(slot_copy, dsend, drecv, d_send, d_recv)
    answer_copy = functools.partial(slot_copy, osend, oret, o_send, o_recv)

    def arrive(copy, e):
        if e == 0:
            copy.wait()
        else:
            copy.wait_recv()

    def last_copy(k, e, a):
        to_core = flip(core, e // 2)
        to_x = flip(x, e % 2)
        column = x * width + core * half_width + k * HD
        start = to_core * dec_count + to_x * rows
        args = (
            fin_v.at[k, pl.ds(pl.multiple_of(start, rows), rows), a * HD : (a + 1) * HD],
            (att_out, qg_out)[a].at[:, pl.ds(pl.multiple_of(column, HD), HD)],
        )
        if e == 0:
            return pltpu.make_async_copy(*args, g_recv.at[k, e, a])
        return pltpu.make_async_remote_copy(
            src_ref=args[0],
            dst_ref=args[1],
            send_sem=g_send.at[k, e, a],
            recv_sem=g_recv.at[k, e, a],
            device_id={"section": section_of(z, y, to_core), "tensor": to_x},
            device_id_type=MESH,
        )

    def last_arrival(k, e, a):
        from_core = flip(core, e // 2)
        from_x = flip(x, e % 2)
        column = from_x * width + from_core * half_width + k * HD
        start = core * dec_count + x * rows
        return pltpu.make_async_remote_copy(
            src_ref=fin_v.at[
                k, pl.ds(pl.multiple_of(start, rows), rows), a * HD : (a + 1) * HD
            ],
            dst_ref=(att_out, qg_out)[a].at[:, pl.ds(pl.multiple_of(column, HD), HD)],
            send_sem=g_send.at[k, e, a],
            recv_sem=g_recv.at[k, e, a],
            device_id={"section": section_of(z, y, from_core), "tensor": from_x},
            device_id_type=MESH,
        )

    for k in range(2):
        exchange(k)
    for copy in scalar_copies:
        copy.wait()

    for n in range(2 * ZS):
        source = section_of(n // 2, y, n % 2)
        start = jnp.int32(0)
        for i in range(PARTNERS):
            pre[n, i] = start
            start = start + dec_len[i, source]
        pre[n, PARTNERS] = start

    OUT_LEN, OUT_AT, OUT_FROM, IN_LEN, IN_AT, IN_FROM = range(6)
    for d in range(2):
        out_at, in_at = jnp.int32(0), jnp.int32(0)
        for n in range(2 * ZS):
            zs = n // 2
            if d == 0:
                begin = pre[n, 2 * z + 2]
                out_len = jnp.where(zs <= z, dec_count - begin, 0)
                first = pre[n, 2 * z]
                in_len = jnp.where(zs < z, dec_count - first, 0)
            else:
                begin, first = jnp.int32(0), jnp.int32(0)
                out_len = jnp.where(zs >= z, pre[n, 2 * z], 0)
                in_len = jnp.where(zs > z, pre[n, 2 * z + 2], 0)
            for name, value in (
                (OUT_LEN, out_len),
                (OUT_AT, out_at),
                (OUT_FROM, begin),
                (IN_LEN, in_len),
                (IN_AT, in_at),
                (IN_FROM, first),
            ):
                seg[d * 6 + name, n] = value
            out_at, in_at = out_at + out_len, in_at + in_len

    def part(d, name, n):
        return seg[d * 6 + name, n]

    def goal_of(count, pieces):
        position = iota((count, 1), 0)
        goal = jnp.full((count, 1), -1, jnp.int32)
        for at, length, column in pieces:
            within = position - at
            goal = jnp.where((within >= 0) & (within < length), within + column, goal)
        return goal

    for d in range(2):
        pieces = []
        for n in range(2 * ZS):
            zs, s = n // 2, n % 2
            column = jnp.where(
                zs == z,
                cap + s * dec_count + part(d, OUT_FROM, n),
                part(d, IN_AT, n) + part(d, OUT_FROM, n) - part(d, IN_FROM, n),
            )
            pieces.append((part(d, OUT_AT, n), part(d, OUT_LEN, n), column))
        fwd_m[d] = one_hot(iota((cap, cap + 2 * dec_count), 1) == goal_of(cap, pieces))

    @pl.when(~has_left)
    def _():
        inc[:, 0] = jnp.zeros(inc.shape[:1] + inc.shape[2:], BF16)
        rin[:, 1] = jnp.zeros(rin.shape[:1] + rin.shape[2:], BF16)

    @pl.when(~has_right)
    def _():
        inc[:, 1] = jnp.zeros(inc.shape[:1] + inc.shape[2:], BF16)
        rin[:, 0] = jnp.zeros(rin.shape[:1] + rin.shape[2:], BF16)

    def build_slots():
        for e in range(4):
            yy, s = flip(y, e // 2), 1 - flip(core, e % 2)
            i = 2 * z + yy
            at = slice(e * DEC_MAX, (e + 1) * DEC_MAX)
            for j in range(ZS - 1):
                zs = j + jnp.where(j >= z, 1, 0)
                n = zs * 2 + s
                d6 = jnp.where(zs < z, 0, 6)
                column = seg[d6 + IN_AT, n] + pre[n, i] - seg[d6 + IN_FROM, n]
                within = iota((DEC_MAX, cap), 0)
                hits = iota((DEC_MAX, cap), 1) - within == column
                hits = hits & (within < pre[n, i + 1] - pre[n, i])
                slot_m[j, at] = one_hot(hits)
            n = z * 2 + s
            column = s * dec_count + pre[n, i]
            within = iota((DEC_MAX, 2 * dec_count), 0)
            hits = iota((DEC_MAX, 2 * dec_count), 1) - within == column
            hits = hits & (within < pre[n, i + 1] - pre[n, i])
            ownslot_m[at] = one_hot(hits)

    def build_examples():
        for t in range(PARTNERS):
            ey, j = t // ZS, t % ZS
            zs = z if j == ZS - 1 else j + jnp.where(j >= z, 1, 0)
            reader = section_of(zs, flip(y, ey), 1 - core)
            start, begin, size = jnp.int32(0), jnp.int32(0), jnp.int32(0)
            for i in range(PARTNERS):
                length = enc_len[i, me]
                match = readers[i, me] == reader
                begin = jnp.where(match, start, begin)
                size = jnp.where(match, length, size)
                start = start + length
            meta[0, t] = begin
            meta[1, t] = size
        mem_f[:, :, enc_count:] = jnp.zeros((2, 2, ENC_MAX, HD), F32)
        pieces = [(meta[0, t], meta[1, t], t * ENC_MAX) for t in range(PARTNERS)]
        goal = goal_of(enc_count, pieces)
        for b in range(enc_count // 256):
            at = slice(b * 256, (b + 1) * 256)
            grad_m[at, :] = one_hot(iota((256, PARTNERS * ENC_MAX), 1) == goal[at])

    remote = (ZS - 1) * 4 * DEC_MAX

    def build_returns():
        for d in range(2):
            pieces = []
            for n in range(2 * ZS):
                zs, s = n // 2, n % 2
                valid = part(d, IN_LEN, n) > 0
                shift = part(d, IN_AT, n) - part(d, IN_FROM, n)
                j = zs - jnp.where(zs > z, 1, 0)
                ec = lax.rem(1 - s - core + 2, 2)
                for yy in range(2):
                    e = lax.rem(yy - y + 2, 2) * 2 + ec
                    begin = pre[n, 2 * z + yy]
                    length = jnp.where(valid, pre[n, 2 * z + yy + 1] - begin, 0)
                    pieces.append((shift + begin, length, (j * 4 + e) * DEC_MAX))
                begin = pre[n, 2 * z + 2] if d == 0 else jnp.int32(0)
                length = dec_count - begin if d == 0 else pre[n, 2 * z]
                column = remote + part(d, OUT_AT, n)
                pieces.append((shift + begin, jnp.where(valid, length, 0), column))
            ret_m[d] = one_hot(iota((cap, remote + cap), 1) == goal_of(cap, pieces))

        pieces = []
        local = 4 * DEC_MAX
        for s in range(2):
            n = z * 2 + s
            ec = lax.rem(1 - s - core + 2, 2)
            for yy in range(2):
                e = lax.rem(yy - y + 2, 2) * 2 + ec
                begin = pre[n, 2 * z + yy]
                length = pre[n, 2 * z + yy + 1] - begin
                pieces.append((s * dec_count + begin, length, e * DEC_MAX))
            begin = pre[n, 2 * z + 2]
            at = s * dec_count
            pieces.append((at + begin, dec_count - begin, local + seg[OUT_AT, n]))
            pieces.append((at, pre[n, 2 * z], local + cap + seg[6 + OUT_AT, n]))
        count = 2 * dec_count
        fin_m[...] = one_hot(iota((count, local + 2 * cap), 1) == goal_of(count, pieces))

    def forward(k, d, starts):
        ring = lax.rem(k, RING)

        @pl.when(k >= RING)
        def _():
            forward_copy(k - RING, d).wait_send()

        @pl.when(jnp.logical_not(starts))
        def _():
            forward_copy(k, d).wait_recv()
            block = matmul(fwd_m[d, :, :cap], inc[k, d], NN)
            block = block + matmul(fwd_m[d, :, cap:], own[k], NN)
            out[ring, d] = block.astype(BF16)

        @pl.when(starts)
        def _():
            out[ring, d] = matmul(fwd_m[d, :, cap:], own[k], NN).astype(BF16)

        forward_copy(k, d).start()

    def deliver(k):
        ring = lax.rem(k, RING)

        @pl.when(z == ZS - 1)
        def _():
            forward_copy(k, 0).wait_recv()

        @pl.when(z == 0)
        def _():
            forward_copy(k, 1).wait_recv()

        @pl.when(k >= RING)
        def _():
            for e in range(1, 4):
                deliver_copy(k - RING, e).wait_send()

        for j in range(ZS - 1):
            d = jnp.where(j < z, 0, 1)
            block = matmul(slot_m[j], inc[k, d], NN).astype(BF16)
            dsend[ring, j] = block.reshape(4, DEC_MAX, 2 * HD)
        block = matmul(ownslot_m[...], own[k], NN).astype(BF16)
        dsend[ring, ZS - 1] = block.reshape(4, DEC_MAX, 2 * HD)
        for e in (3, 2, 1, 0):
            deliver_copy(k, e).start()

    def attend(k):
        ring = lax.rem(k, RING)
        pair = lax.rem(k, 2)
        for ec in range(2):
            memory_copy(k, ec).wait()
        for a in range(2):
            for ec in range(2):
                at = slice(ec * HD, (ec + 1) * HD)
                mem_f[a, ec, :enc_count] = mem_v[pair, a, :, at].astype(F32)

        @pl.when(k + 2 < chunks)
        def _():
            for ec in range(2):
                memory_copy(k + 2, ec).start()

        @pl.when(k >= RING)
        def _():
            for e in range(1, 4):
                answer_copy(k - RING, e).wait_send()

        for e in range(4):
            arrive(deliver_copy(k, e), e)

        @pl.loop(0, 2)
        def _(ey):
            units = [(ey * ZS + j, j, ec) for j in range(ZS) for ec in range(2)]
            column = iota((DEC_MAX, ENC_MAX), 1)

            def tokens(unit, a):
                t, j, ec = unit
                return drecv[k, j, ey * 2 + ec, :, a * HD : (a + 1) * HD]

            def example(unit, a):
                t, j, ec = unit
                return mem_f[a, ec, pl.ds(meta[0, t], ENC_MAX)].astype(BF16)

            keys = [example(unit, 0) for unit in units]
            values = [example(unit, 1) for unit in units]
            scores = [matmul(tokens(u, 0), key, NT) for u, key in zip(units, keys)]
            dprobs = [matmul(tokens(u, 1), value, NT) for u, value in zip(units, values)]
            scores = [jnp.where(column < meta[1, u[0]], s, -jnp.inf) for u, s in zip(units, scores)]
            most = [jnp.max(s, axis=1, keepdims=True) for s in scores]
            weights = [jnp.exp((s - m) * scaling) for s, m in zip(scores, most)]
            scale = [1.0 / jnp.sum(w, axis=1, keepdims=True) for w in weights]
            probs = [w * r for w, r in zip(weights, scale)]
            delta = [jnp.sum(w * d, axis=1, keepdims=True) for w, d in zip(probs, dprobs)]
            low = [w.astype(BF16) for w in probs]
            dscores = [
                (w * (d - e)).astype(BF16) for w, d, e in zip(probs, dprobs, delta)
            ]
            for i, (t, j, ec) in enumerate(units):
                e = ey * 2 + ec
                at = slice(ec * HD, (ec + 1) * HD)
                osend[ring, j, e, :, :HD] = matmul(low[i], values[i], NN).astype(BF16)
                block = matmul(dscores[i], keys[i], NN) * scaling
                osend[ring, j, e, :, HD:] = block.astype(BF16)
                block = matmul(dscores[i], tokens(units[i], 0), TN) * scaling
                d_x[0, t, :, at] = block.astype(BF16)
                d_x[1, t, :, at] = matmul(low[i], tokens(units[i], 1), TN).astype(BF16)

        for e in (3, 2, 1, 0):
            answer_copy(k, e).start()

    def collect(k):
        pair = lax.rem(k, 2)

        @pl.when(k >= 2)
        def _():
            for ec in range(2):
                gradient_copy(k - 2, ec).wait()

        for a in range(2):

            @pl.loop(0, enc_count // 256)
            def _(b):
                at = pl.ds(pl.multiple_of(b * 256, 256), 256)
                block = d_x[a].reshape(PARTNERS * ENC_MAX, 2 * HD)
                mg_v[pair, a, at] = matmul(grad_m[at, :], block, NN).astype(BF16)

        for ec in range(2):
            gradient_copy(k, ec).start()

    def answers(k):
        for e in range(4):
            arrive(answer_copy(k, e), e)

    def give_back(k, d, starts):
        ring = lax.rem(k, RING)

        @pl.when(k >= RING)
        def _():
            return_copy(k - RING, d).wait_send()

        answered = oret[k, : ZS - 1].reshape(remote, 2 * HD)

        @pl.when(jnp.logical_not(starts))
        def _():
            return_copy(k, d).wait_recv()
            block = matmul(ret_m[d, :, :remote], answered, NN)
            block = block + matmul(ret_m[d, :, remote:], rin[k, d], NN)
            rout[ring, d] = block.astype(BF16)

        @pl.when(starts)
        def _():
            rout[ring, d] = matmul(ret_m[d, :, :remote], answered, NN).astype(BF16)

        return_copy(k, d).start()

    def finish(k):
        @pl.when(z == 0)
        def _():
            return_copy(k, 0).wait_recv()

        @pl.when(z == ZS - 1)
        def _():
            return_copy(k, 1).wait_recv()

        local = 4 * DEC_MAX
        block = matmul(fin_m[:, :local], oret[k, ZS - 1].reshape(local, 2 * HD), NN)
        for d in range(2):
            at = local + d * cap
            block = block + matmul(fin_m[:, at : at + cap], rin[k, d], NN)
        fin_v[k] = block.astype(BF16)
        for e in (3, 2, 1, 0):
            for a in range(2):
                last_copy(k, e, a).start()

    for k in range(2):
        for ec in range(2):
            memory_copy(k, ec).start()

    near = ZS - 1
    lag = 1
    back = lag * near + 2
    settled = lag * far + jnp.where(far < near, 3, 2)
    steps = chunks + back + lag * near

    def during(k, condition=None):
        go = (k >= 0) & (k < chunks)
        if condition is not None:
            go = go & condition
        return pl.when(go)

    @pl.loop(0, steps)
    def _(t):
        @during(t)
        def _():
            for e in range(4):
                for a in range(2):
                    arrive(exchange_copy(t, e, a), e)

            @pl.when(t + 2 < chunks)
            def _():
                exchange(t + 2)

        @during(t - lag * z, has_right)
        def _():
            forward(t - lag * z, 0, z == 0)

        @during(t - lag * (near - z), has_left)
        def _():
            forward(t - lag * (near - z), 1, z == near)

        @pl.when(t == 0)
        def _():
            build_slots()
            build_examples()
            build_returns()

        @during(t - lag * far)
        def _():
            deliver(t - lag * far)

        @during(t - settled)
        def _():
            answers(t - settled)

        @during(t - back - lag * (near - z), has_left)
        def _():
            give_back(t - back - lag * (near - z), 0, z == near)

        @during(t - back - lag * z, has_right)
        def _():
            give_back(t - back - lag * z, 1, z == 0)

        @during(t - lag * far - 1)
        def _():
            attend(t - lag * far - 1)

        @during(t - lag * far - 1)
        def _():
            collect(t - lag * far - 1)

        @during(t - back - lag * far)
        def _():
            finish(t - back - lag * far)

    @pl.loop(0, chunks)
    def _(k):
        for e in range(4):
            for a in range(2):
                if e == 0:
                    last_copy(k, e, a).wait()
                else:
                    exchange_copy(k, e, a).wait_send()
                    last_copy(k, e, a).wait_send()
                    last_arrival(k, e, a).wait_recv()

    @pl.loop(chunks - RING, chunks)
    def _(k):
        for e in range(1, 4):
            deliver_copy(k, e).wait_send()
            answer_copy(k, e).wait_send()

        @pl.when(has_right)
        def _():
            forward_copy(k, 0).wait_send()
            return_copy(k, 1).wait_send()

        @pl.when(has_left)
        def _():
            forward_copy(k, 1).wait_send()
            return_copy(k, 0).wait_send()

    @pl.loop(chunks - 2, chunks)
    def _(k):
        for ec in range(2):
            gradient_copy(k, ec).wait()


def packed_body(memory, queries, out_grad, enc_lengths, dec_lengths, readers):
    enc_count, width = memory.shape[1:]
    rows = queries.shape[0]
    count = 4 * rows
    chunks = width // 2 // HD
    pair = 2 * HD
    scalars = (enc_lengths.T, dec_lengths.T, readers.T)
    anywhere = pl.BlockSpec(memory_space=pl.ANY)
    dma = pltpu.SemaphoreType.DMA
    blocks = (ZS, 4, DEC_MAX, pair)
    local = 4 * DEC_MAX
    remote = (ZS - 1) * local

    def vmem(*shape):
        return pltpu.VMEM(shape, BF16)

    return pl.pallas_call(
        packed_kernel,
        out_shape=(
            jax.ShapeDtypeStruct(queries.shape, BF16),
            jax.ShapeDtypeStruct(queries.shape, BF16),
            jax.ShapeDtypeStruct(memory.shape, BF16),
        ),
        in_specs=[anywhere] * 6,
        out_specs=(anywhere,) * 3,
        scratch_shapes=[
            vmem(chunks, count, pair),
            vmem(chunks, 2, CAP, pair),
            vmem(RING, 2, CAP, pair),
            vmem(RING, *blocks),
            vmem(chunks, *blocks),
            vmem(RING, *blocks),
            vmem(chunks, *blocks),
            vmem(chunks, 2, CAP, pair),
            vmem(RING, 2, CAP, pair),
            vmem(chunks, count, pair),
            vmem(2, 2, enc_count, pair),
            vmem(2, 2, enc_count, pair),
            pltpu.VMEM((2, 2, enc_count + ENC_MAX, HD), F32),
            vmem(2, PARTNERS, ENC_MAX, pair),
            vmem(2, CAP, CAP + count),
            vmem(ZS - 1, local, CAP),
            vmem(local, count),
            vmem(2, CAP, remote + CAP),
            vmem(count, local + 2 * CAP),
            vmem(enc_count, PARTNERS * ENC_MAX),
            *[pltpu.SMEM(array.shape, jnp.int32) for array in scalars],
            pltpu.SMEM((2 * ZS, PARTNERS + 1), jnp.int32),
            pltpu.SMEM((12, 2 * ZS), jnp.int32),
            pltpu.SMEM((2, PARTNERS), jnp.int32),
            dma((chunks, 4, 2)),
            dma((chunks, 4, 2)),
            dma((RING, 2)),
            dma((chunks, 2)),
            dma((RING, 4)),
            dma((chunks, 4)),
            dma((RING, 4)),
            dma((chunks, 4)),
            dma((RING, 2)),
            dma((chunks, 2)),
            dma((chunks, 4, 2)),
            dma((chunks, 4, 2)),
            dma((2, 2)),
            dma((2, 2)),
            dma((3,)),
        ],
        compiler_params=pltpu.CompilerParams(
            collective_id=1, has_side_effects=True, vmem_limit_bytes=60 * 1024 * 1024
        ),
    )(memory, queries, out_grad, *scalars)


def most_rows(dec_lengths):
    place = np.arange(2 * ZS * 2 * 2 * ZS).reshape(4 * ZS, 2 * ZS)
    source, half = place // (8 * ZS), place // (4 * ZS) % 2
    goal = place % (2 * ZS) // 2
    blocks = []
    for cut in range(1, ZS):
        for y in range(2):
            blocks.append((half == y) & (source < cut) & (goal >= cut))
            blocks.append((half == y) & (source >= cut) & (goal < cut))
    counts = jnp.where(np.stack(blocks), dec_lengths, 0)
    return jnp.max(jnp.sum(counts, axis=(1, 2)))


def body(sections, tensors, *args):
    packs = (sections, tensors) == (4 * ZS, 2)
    padded = functools.partial(padded_body, sections, tensors, packs)
    if not packs:
        return padded(*args)
    return lax.cond(most_rows(args[4]) <= CAP, packed_body, padded, *args)


def solution(mesh):
    placed = (
        P(None, "section", "tensor"),
        P(("section", "tensor"), None),
        P(("section", "tensor"), None),
        P(),
        P(),
        P(),
    )
    return jax.shard_map(
        functools.partial(body, mesh.shape["section"], mesh.shape["tensor"]),
        mesh=mesh,
        in_specs=placed,
        out_specs=(
            P(("section", "tensor"), None),
            P(("section", "tensor"), None),
            P(None, "section", "tensor"),
        ),
        check_vma=False,
    )
```

```python
import functools

import jax
import jax.numpy as jnp
import numpy as np
from jax import lax
from jax.experimental import pallas as pl
from jax.experimental.pallas import tpu as pltpu
from jax.sharding import PartitionSpec as P

HD = 128
ENC_MAX = 128
DEC_MAX = 64
PARTNERS = 8
MOST_CHUNKS = 8
BF16 = jnp.bfloat16
F32 = jnp.float32
MESH = pl.DeviceIdType.MESH


def matmul(a, b, dims):
    return lax.dot_general(a, b, (dims, ((), ())), preferred_element_type=F32)


NN = ((1,), (0,))
NT = ((1,), (1,))
TN = ((0,), (0,))


def chunk_count(width):
    return min(MOST_CHUNKS, width // HD)


def staged_kernel(sections, tensors, *refs):
    inputs, results, staging = refs[:6], refs[6:9], refs[9:12]
    sem = refs[-1]
    kernel(sections, tensors, *inputs, *staging, *refs[12:-1])
    copies = [
        pltpu.make_async_copy(source, target, sem.at[i])
        for i, (source, target) in enumerate(zip(staging, results))
    ]
    for copy in copies:
        copy.start()
    for copy in copies:
        copy.wait()


def kernel(
    sections,
    tensors,
    mem_hbm,
    q_hbm,
    g_hbm,
    enc_hbm,
    dec_hbm,
    readers_hbm,
    att_out,
    qg_out,
    mg_out,
    mem_v,
    dec_v,
    fsend,
    frecv,
    osend,
    oret,
    fin_v,
    kv_x,
    d_x,
    pack_m,
    unpack_m,
    enc_m,
    grad_m,
    enc_len,
    dec_len,
    readers,
    meta,
    a_send,
    a_recv,
    a_local,
    f_send,
    f_recv,
    o_send,
    o_recv,
    g_send,
    g_recv,
    g_local,
    m_in,
    s_in,
):
    me = lax.axis_index("section")
    mine = lax.axis_index("tensor")
    rows = q_hbm.shape[0]
    enc_count = mem_v.shape[1]
    dec_count = dec_v.shape[2]
    width = mem_v.shape[2]
    chunks = chunk_count(width)
    piece = width // chunks
    spacing = sections // PARTNERS
    scaling = HD ** (-0.5)

    def holder_of(slot):
        return lax.rem(me + 2 * sections - slot * spacing - 1, sections)

    def reader_of(slot):
        return lax.rem(me + slot * spacing + 1, sections)

    half = PARTNERS // 2

    def peer_of(step):
        return lax.rem(mine + step, tensors)

    mem_copy = pltpu.make_async_copy(mem_hbm, mem_v, m_in)
    scalar_copies = [
        pltpu.make_async_copy(source, target, s_in.at[i])
        for i, (source, target) in enumerate(
            ((enc_hbm, enc_len), (dec_hbm, dec_len), (readers_hbm, readers))
        )
    ]
    for copy in scalar_copies:
        copy.start()

    barrier = pltpu.get_barrier_semaphore()
    for step in range(1, tensors):
        pl.semaphore_signal(
            barrier, inc=1, device_id={"tensor": peer_of(step)}, device_id_type=MESH
        )
    for slot in range(PARTNERS):
        pl.semaphore_signal(
            barrier, inc=1, device_id={"section": holder_of(slot)}, device_id_type=MESH
        )
        pl.semaphore_signal(
            barrier, inc=1, device_id={"section": reader_of(slot)}, device_id_type=MESH
        )
    pl.semaphore_wait(barrier, tensors - 1 + 2 * PARTNERS)

    own_rows = pl.ds(pl.multiple_of(mine * rows, rows), rows)

    def first_copy(c, a, step):
        peer = peer_of(step)
        source = (q_hbm, g_hbm)[a]
        columns = pl.ds(pl.multiple_of(peer * width + c * piece, piece), piece)
        if step == 0:
            return pltpu.make_async_copy(
                source.at[:, columns], dec_v.at[c, a, own_rows], a_local.at[c, a]
            )
        return pltpu.make_async_remote_copy(
            src_ref=source.at[:, columns],
            dst_ref=dec_v.at[c, a, own_rows],
            send_sem=a_send.at[c, a, step - 1],
            recv_sem=a_recv.at[c, a, step - 1],
            device_id={"tensor": peer},
            device_id_type=MESH,
        )

    def fetch(c):
        for a in range(2):
            for step in list(range(1, tensors)) + [0]:
                first_copy(c, a, step).start()

    fetch(0)
    mem_copy.start()
    for copy in scalar_copies:
        copy.wait()

    start = jnp.int32(0)
    for i in range(PARTNERS):
        length = dec_len[i, me]
        meta[0, i] = start
        meta[1, i] = length
        start = start + length
    for slot in range(PARTNERS):
        reader = reader_of(slot)
        start, begin, size = jnp.int32(0), jnp.int32(0), jnp.int32(0)
        for j in range(PARTNERS):
            length = enc_len[j, me]
            match = readers[j, me] == reader
            begin = jnp.where(match, start, begin)
            size = jnp.where(match, length, size)
            start = start + length
        meta[2, slot] = begin
        meta[3, slot] = size

    def one_hot(hits):
        return jnp.where(hits, 1.0, 0.0).astype(BF16)

    def iota(shape, dim):
        return lax.broadcasted_iota(jnp.int32, shape, dim)

    for i in range(PARTNERS):
        shape = (DEC_MAX, dec_count)
        within = iota(shape, 0)
        hits = (iota(shape, 1) - within == meta[0, i]) & (within < meta[1, i])
        pack_m[i // half, (i % half) * DEC_MAX : (i % half + 1) * DEC_MAX, :] = one_hot(hits)

    def forward_copy(c, slot):
        holder = holder_of(slot)
        return pltpu.make_async_remote_copy(
            src_ref=fsend.at[c, :, lax.div(holder, spacing)],
            dst_ref=frecv.at[c, :, slot],
            send_sem=f_send.at[c, slot],
            recv_sem=f_recv.at[c, slot],
            device_id={"section": holder},
            device_id_type=MESH,
        )

    def back_copy(c, slot):
        return pltpu.make_async_remote_copy(
            src_ref=osend.at[c, :, slot],
            dst_ref=oret.at[c, :, lax.div(me, spacing)],
            send_sem=o_send.at[c, slot],
            recv_sem=o_recv.at[c, lax.div(me, spacing)],
            device_id={"section": reader_of(slot)},
            device_id_type=MESH,
        )

    def back_arrival(c, i):
        return pltpu.make_async_remote_copy(
            src_ref=osend.at[c, :, i],
            dst_ref=oret.at[c, :, i],
            send_sem=o_send.at[c, i],
            recv_sem=o_recv.at[c, i],
            device_id={"section": reader_of(i)},
            device_id_type=MESH,
        )

    def last_copy(c, a, step):
        peer = peer_of(step)
        target = (att_out, qg_out)[a]
        source = fin_v.at[c, a, pl.ds(pl.multiple_of(peer * rows, rows), rows)]
        columns = pl.ds(pl.multiple_of(mine * width + c * piece, piece), piece)
        if step == 0:
            return pltpu.make_async_copy(source, target.at[:, columns], g_local.at[c, a])
        return pltpu.make_async_remote_copy(
            src_ref=source,
            dst_ref=target.at[:, columns],
            send_sem=g_send.at[c, a, step - 1],
            recv_sem=g_recv.at[c, a, step - 1],
            device_id={"tensor": peer},
            device_id_type=MESH,
        )

    def pack(c):
        for a in range(2):
            first_copy(c, a, 0).wait()
            for step in range(1, tensors):
                first_copy(c, a, step).wait_recv()
        if c + 1 < chunks:
            fetch(c + 1)
        for a in range(2):
            for g in range(2):
                block = matmul(pack_m[g], dec_v[c, a], NN).astype(BF16)
                fsend[c, a, g * half : (g + 1) * half] = block.reshape(half, DEC_MAX, piece)

        @pl.loop(0, PARTNERS)
        def _(turn):
            forward_copy(c, turn).start()

    def expand(c):
        @pl.loop(0, PARTNERS // 2)
        def _(g):
            for a in range(2):
                block = matmul(enc_m[g], mem_v[a, :, c * piece : (c + 1) * piece], NN)
                kv_x[c, a, pl.ds(g * 2, 2)] = block.astype(BF16).reshape(2, ENC_MAX, piece)

    def attend(c):
        @pl.loop(0, PARTNERS)
        def _(turn):
            slot = turn
            forward_copy(c, slot).wait_recv()
            valid = iota((DEC_MAX, ENC_MAX), 1) < meta[3, slot]
            for h in range(piece // HD):
                at = slice(h * HD, (h + 1) * HD)
                q = frecv[c, 0, slot, :, at]
                g = frecv[c, 1, slot, :, at]
                k = kv_x[c, 0, slot, :, at]
                v = kv_x[c, 1, slot, :, at]
                scores = jnp.where(valid, matmul(q, k, NT) * scaling, -jnp.inf)
                weights = jnp.exp(scores - jnp.max(scores, axis=1, keepdims=True))
                probs = weights / jnp.sum(weights, axis=1, keepdims=True)
                low = probs.astype(BF16)
                dprobs = matmul(g, v, NT)
                delta = jnp.sum(probs * dprobs, axis=1, keepdims=True)
                dscores = (probs * (dprobs - delta)).astype(BF16)
                osend[c, 0, slot, :, at] = matmul(low, v, NN).astype(BF16)
                osend[c, 1, slot, :, at] = (matmul(dscores, k, NN) * scaling).astype(BF16)
                d_x[0, slot, :, at] = (matmul(dscores, q, TN) * scaling).astype(BF16)
                d_x[1, slot, :, at] = matmul(low, g, TN).astype(BF16)
            back_copy(c, slot).start()

    def collect(c):
        @pl.loop(0, enc_count // 256)
        def _(b):
            at = pl.ds(pl.multiple_of(b * 256, 256), 256)
            for a in range(2):
                block = d_x[a].reshape(PARTNERS * ENC_MAX, piece)
                mg_out[a, at, c * piece : (c + 1) * piece] = matmul(
                    grad_m[at, :], block, NN
                ).astype(BF16)

    def finish(c):
        @pl.loop(0, PARTNERS)
        def _(i):
            back_arrival(c, i).wait_recv()

        for a in range(2):
            block = oret[c, a].reshape(PARTNERS * DEC_MAX, piece)
            fin_v[c, a] = matmul(unpack_m[...], block, NN).astype(BF16)
            for step in list(range(1, tensors)) + [0]:
                last_copy(c, a, step).start()

    def settle():
        for c in range(chunks):
            for a in range(2):
                for step in range(1, tensors):
                    first_copy(c, a, step).wait_send()

            @pl.loop(0, PARTNERS)
            def _(slot):
                forward_copy(c, slot).wait_send()
                back_copy(c, slot).wait_send()

    pack(0)

    for slot in range(PARTNERS):
        shape = (ENC_MAX, enc_count)
        within = iota(shape, 0)
        hits = (iota(shape, 1) - within == meta[2, slot]) & (within < meta[3, slot])
        enc_m[slot // 2, (slot % 2) * ENC_MAX : (slot % 2 + 1) * ENC_MAX, :] = one_hot(hits)
    mem_copy.wait()
    expand(0)
    pack(1)

    position = iota((dec_count, 1), 0)
    goal = jnp.full((dec_count, 1), -1, jnp.int32)
    for i in range(PARTNERS):
        within = position - meta[0, i]
        goal = jnp.where((within >= 0) & (within < meta[1, i]), within + i * DEC_MAX, goal)
    unpack_m[...] = one_hot(iota((dec_count, PARTNERS * DEC_MAX), 1) == goal)
    for b in range(enc_count // 256):
        position = iota((256, 1), 0) + b * 256
        goal = jnp.full((256, 1), -1, jnp.int32)
        for slot in range(PARTNERS):
            within = position - meta[2, slot]
            goal = jnp.where(
                (within >= 0) & (within < meta[3, slot]), within + slot * ENC_MAX, goal
            )
        hits = iota((256, PARTNERS * ENC_MAX), 1) == goal
        grad_m[b * 256 : (b + 1) * 256, :] = one_hot(hits)

    expand(1)
    for c in range(2, chunks):
        pack(c)
        expand(c)
    for c in range(chunks):
        attend(c)
        collect(c)
        if c >= 3:
            finish(c - 3)
    for c in range(max(chunks - 3, 0), chunks):
        if c == chunks - 1:
            settle()
        finish(c)

    for c in range(chunks):
        for a in range(2):
            for step in range(1, tensors):
                last_copy(c, a, step).wait()
            last_copy(c, a, 0).wait()


def padded_body(sections, tensors, staged, memory, queries, out_grad, enc_lengths, dec_lengths, readers):
    enc_count, width = memory.shape[1:]
    rows = queries.shape[0]
    dec_count = rows * tensors
    chunks = chunk_count(width)
    piece = width // chunks
    blocks = (chunks, 2, PARTNERS, DEC_MAX, piece)
    peers = max(tensors - 1, 1)
    scalars = (enc_lengths.T, dec_lengths.T, readers.T)
    anywhere = pl.BlockSpec(memory_space=pl.ANY)
    resident = pl.BlockSpec(memory_space=pltpu.VMEM)
    results = [array.shape for array in (queries, queries, memory)]
    dma = pltpu.SemaphoreType.DMA
    return pl.pallas_call(
        functools.partial(staged_kernel if staged else kernel, sections, tensors),
        out_shape=tuple(
            jax.ShapeDtypeStruct(shape, BF16) if staged else pltpu.VMEM(shape, BF16)
            for shape in results
        ),
        in_specs=[anywhere] * 6,
        out_specs=(anywhere if staged else resident,) * 3,
        scratch_shapes=[
            *[pltpu.VMEM(shape, BF16) for shape in results if staged],
            pltpu.VMEM((2, enc_count, width), BF16),
            pltpu.VMEM((chunks, 2, dec_count, piece), BF16),
            pltpu.VMEM(blocks, BF16),
            pltpu.VMEM(blocks, BF16),
            pltpu.VMEM(blocks, BF16),
            pltpu.VMEM(blocks, BF16),
            pltpu.VMEM((chunks, 2, dec_count, piece), BF16),
            pltpu.VMEM((chunks, 2, PARTNERS, ENC_MAX, piece), BF16),
            pltpu.VMEM((2, PARTNERS, ENC_MAX, piece), BF16),
            pltpu.VMEM((2, PARTNERS // 2 * DEC_MAX, dec_count), BF16),
            pltpu.VMEM((dec_count, PARTNERS * DEC_MAX), BF16),
            pltpu.VMEM((PARTNERS // 2, 2 * ENC_MAX, enc_count), BF16),
            pltpu.VMEM((enc_count, PARTNERS * ENC_MAX), BF16),
            *[pltpu.SMEM(array.shape, jnp.int32) for array in scalars],
            pltpu.SMEM((4, PARTNERS), jnp.int32),
            dma((chunks, 2, peers)),
            dma((chunks, 2, peers)),
            dma((chunks, 2)),
            dma((chunks, PARTNERS)),
            dma((chunks, PARTNERS)),
            dma((chunks, PARTNERS)),
            dma((chunks, PARTNERS)),
            dma((chunks, 2, peers)),
            dma((chunks, 2, peers)),
            dma((chunks, 2)),
            dma,
            dma((3,)),
            *[dma((3,))] * staged,
        ],
        compiler_params=pltpu.CompilerParams(
            collective_id=0, has_side_effects=True, vmem_limit_bytes=(56 if staged else 46) * 1024 * 1024
        ),
    )(memory, queries, out_grad, *scalars)


ZS = 4
CAP = 640
OUTER = 544


class Hop:
    def __init__(self, make, middle):
        self.make, self.middle = make, middle

    def each(self, action):
        @pl.when(self.middle)
        def _():
            action(self.make(CAP))

        @pl.when(jnp.logical_not(self.middle))
        def _():
            action(self.make(OUTER))

    def start(self):
        self.each(lambda copy: copy.start())

    def wait_send(self):
        self.each(lambda copy: copy.wait_send())

    def wait_recv(self):
        self.each(lambda copy: copy.wait_recv())


RING = 4


def packed_kernel(
    mem_hbm,
    q_hbm,
    g_hbm,
    enc_hbm,
    dec_hbm,
    readers_hbm,
    att_out,
    qg_out,
    mg_out,
    own,
    inc,
    out,
    dsend,
    drecv,
    osend,
    oret,
    rin,
    rout,
    fin_v,
    mem_v,
    mg_v,
    mem_f,
    d_x,
    fwd_m,
    slot_m,
    ownslot_m,
    ret_m,
    fin_m,
    grad_m,
    enc_len,
    dec_len,
    readers,
    pre,
    seg,
    meta,
    a_send,
    a_recv,
    f_send,
    f_recv,
    d_send,
    d_recv,
    o_send,
    o_recv,
    r_send,
    r_recv,
    g_send,
    g_recv,
    m_in,
    m_out,
    s_in,
):
    me = lax.axis_index("section")
    x = lax.axis_index("tensor")
    z = lax.div(me, 4)
    y = lax.rem(lax.div(me, 2), 2)
    core = lax.rem(me, 2)
    rows = q_hbm.shape[0]
    dec_count = 2 * rows
    enc_count = mem_hbm.shape[1]
    width = mem_hbm.shape[2]
    half_width = width // 2
    chunks = half_width // HD
    cap = inc.shape[2]
    scaling = HD ** (-0.5)
    has_right = z < ZS - 1
    has_left = z > 0
    far = jnp.maximum(z, ZS - 1 - z)

    def flip(value, step):
        return lax.rem(value + step, 2)

    def section_of(zz, yy, cc):
        return zz * 4 + yy * 2 + cc

    def iota(shape, dim):
        return lax.broadcasted_iota(jnp.int32, shape, dim)

    def one_hot(hits):
        return jnp.where(hits, 1.0, 0.0).astype(BF16)

    scalar_copies = [
        pltpu.make_async_copy(source, target, s_in.at[i])
        for i, (source, target) in enumerate(
            ((enc_hbm, enc_len), (dec_hbm, dec_len), (readers_hbm, readers))
        )
    ]
    for copy in scalar_copies:
        copy.start()

    barrier = pltpu.get_barrier_semaphore()

    def greet(section, tensor):
        pl.semaphore_signal(
            barrier,
            inc=1,
            device_id={"section": section, "tensor": tensor},
            device_id_type=MESH,
        )

    greet(section_of(z, y, core), flip(x, 1))
    greet(section_of(z, y, flip(core, 1)), flip(x, 1))
    for e in range(1, 4):
        greet(section_of(z, flip(y, e // 2), flip(core, e % 2)), x)

    @pl.when(has_right)
    def _():
        greet(me + 4, x)

    @pl.when(has_left)
    def _():
        greet(me - 4, x)

    pl.semaphore_wait(barrier, 5 + jnp.where(has_right, 1, 0) + jnp.where(has_left, 1, 0))

    def exchange_copy(k, e, a):
        to_core = flip(core, e // 2)
        to_x = flip(x, e % 2)
        source = (q_hbm, g_hbm)[a]
        column = to_x * width + to_core * half_width + k * HD
        start = core * dec_count + x * rows
        args = (
            source.at[:, pl.ds(pl.multiple_of(column, HD), HD)],
            own.at[k, pl.ds(pl.multiple_of(start, rows), rows), a * HD : (a + 1) * HD],
        )
        if e == 0:
            return pltpu.make_async_copy(*args, a_recv.at[k, e, a])
        return pltpu.make_async_remote_copy(
            src_ref=args[0],
            dst_ref=args[1],
            send_sem=a_send.at[k, e, a],
            recv_sem=a_recv.at[k, e, a],
            device_id={"section": section_of(z, y, to_core), "tensor": to_x},
            device_id_type=MESH,
        )

    def exchange(k):
        for e in (3, 2, 1, 0):
            for a in range(2):
                exchange_copy(k, e, a).start()

    def memory_copy(k, ec):
        column = flip(core, ec) * half_width + k * HD
        ring = lax.rem(k, 2)
        return pltpu.make_async_copy(
            mem_hbm.at[:, :, pl.ds(pl.multiple_of(column, HD), HD)],
            mem_v.at[ring, :, :, ec * HD : (ec + 1) * HD],
            m_in.at[ring, ec],
        )

    def gradient_copy(k, ec):
        column = flip(core, ec) * half_width + k * HD
        ring = lax.rem(k, 2)
        return pltpu.make_async_copy(
            mg_v.at[ring, :, :, ec * HD : (ec + 1) * HD],
            mg_out.at[:, :, pl.ds(pl.multiple_of(column, HD), HD)],
            m_out.at[ring, ec],
        )

    def forward_copy(k, d, arrives=False):
        ring = lax.rem(k, RING)

        def make(count):
            return pltpu.make_async_remote_copy(
                src_ref=out.at[ring, d, :count],
                dst_ref=inc.at[k, d, :count],
                send_sem=f_send.at[ring, d],
                recv_sem=f_recv.at[k, d],
                device_id={"section": me + (4, -4)[d]},
                device_id_type=MESH,
            )

        return Hop(make, (z == 1, z == 2)[d ^ arrives])

    def return_copy(k, d, arrives=False):
        ring = lax.rem(k, RING)

        def make(count):
            return pltpu.make_async_remote_copy(
                src_ref=rout.at[ring, d, :count],
                dst_ref=rin.at[k, d, :count],
                send_sem=r_send.at[ring, d],
                recv_sem=r_recv.at[k, d],
                device_id={"section": me + (-4, 4)[d]},
                device_id_type=MESH,
            )

        return Hop(make, (z == 2, z == 1)[d ^ arrives])

    def slot_copy(send, recv, send_sem, recv_sem, k, e):
        ring = lax.rem(k, RING)
        if e == 0:
            return pltpu.make_async_copy(
                send.at[ring, :, e], recv.at[k, :, e], recv_sem.at[k, e]
            )
        return pltpu.make_async_remote_copy(
            src_ref=send.at[ring, :, e],
            dst_ref=recv.at[k, :, e],
            send_sem=send_sem.at[ring, e],
            recv_sem=recv_sem.at[k, e],
            device_id={"section": section_of(z, flip(y, e // 2), flip(core, e % 2))},
            device_id_type=MESH,
        )

    deliver_copy = functools.partial(slot_copy, dsend, drecv, d_send, d_recv)
    answer_copy = functools.partial(slot_copy, osend, oret, o_send, o_recv)

    def arrive(copy, e):
        if e == 0:
            copy.wait()
        else:
            copy.wait_recv()

    def last_copy(k, e, a):
        to_core = flip(core, e // 2)
        to_x = flip(x, e % 2)
        column = x * width + core * half_width + k * HD
        start = to_core * dec_count + to_x * rows
        args = (
            fin_v.at[k, pl.ds(pl.multiple_of(start, rows), rows), a * HD : (a + 1) * HD],
            (att_out, qg_out)[a].at[:, pl.ds(pl.multiple_of(column, HD), HD)],
        )
        if e == 0:
            return pltpu.make_async_copy(*args, g_recv.at[k, e, a])
        return pltpu.make_async_remote_copy(
            src_ref=args[0],
            dst_ref=args[1],
            send_sem=g_send.at[k, e, a],
            recv_sem=g_recv.at[k, e, a],
            device_id={"section": section_of(z, y, to_core), "tensor": to_x},
            device_id_type=MESH,
        )

    def last_arrival(k, e, a):
        from_core = flip(core, e // 2)
        from_x = flip(x, e % 2)
        column = from_x * width + from_core * half_width + k * HD
        start = core * dec_count + x * rows
        return pltpu.make_async_remote_copy(
            src_ref=fin_v.at[
                k, pl.ds(pl.multiple_of(start, rows), rows), a * HD : (a + 1) * HD
            ],
            dst_ref=(att_out, qg_out)[a].at[:, pl.ds(pl.multiple_of(column, HD), HD)],
            send_sem=g_send.at[k, e, a],
            recv_sem=g_recv.at[k, e, a],
            device_id={"section": section_of(z, y, from_core), "tensor": from_x},
            device_id_type=MESH,
        )

    for k in range(2):
        exchange(k)
    for copy in scalar_copies:
        copy.wait()

    for n in range(2 * ZS):
        source = section_of(n // 2, y, n % 2)
        start = jnp.int32(0)
        for i in range(PARTNERS):
            pre[n, i] = start
            start = start + dec_len[i, source]
        pre[n, PARTNERS] = start

    OUT_LEN, OUT_AT, OUT_FROM, IN_LEN, IN_AT, IN_FROM = range(6)
    for d in range(2):
        out_at, in_at = jnp.int32(0), jnp.int32(0)
        for n in range(2 * ZS):
            zs = n // 2
            if d == 0:
                begin = pre[n, 2 * z + 2]
                out_len = jnp.where(zs <= z, dec_count - begin, 0)
                first = pre[n, 2 * z]
                in_len = jnp.where(zs < z, dec_count - first, 0)
            else:
                begin, first = jnp.int32(0), jnp.int32(0)
                out_len = jnp.where(zs >= z, pre[n, 2 * z], 0)
                in_len = jnp.where(zs > z, pre[n, 2 * z + 2], 0)
            for name, value in (
                (OUT_LEN, out_len),
                (OUT_AT, out_at),
                (OUT_FROM, begin),
                (IN_LEN, in_len),
                (IN_AT, in_at),
                (IN_FROM, first),
            ):
                seg[d * 6 + name, n] = value
            out_at, in_at = out_at + out_len, in_at + in_len

    def part(d, name, n):
        return seg[d * 6 + name, n]

    def goal_of(count, pieces):
        position = iota((count, 1), 0)
        goal = jnp.full((count, 1), -1, jnp.int32)
        for at, length, column in pieces:
            within = position - at
            goal = jnp.where((within >= 0) & (within < length), within + column, goal)
        return goal

    for d in range(2):
        pieces = []
        for n in range(2 * ZS):
            zs, s = n // 2, n % 2
            column = jnp.where(
                zs == z,
                cap + s * dec_count + part(d, OUT_FROM, n),
                part(d, IN_AT, n) + part(d, OUT_FROM, n) - part(d, IN_FROM, n),
            )
            pieces.append((part(d, OUT_AT, n), part(d, OUT_LEN, n), column))

        @pl.when((has_right, has_left)[d])
        def _():
            hits = iota((cap, cap + 2 * dec_count), 1) == goal_of(cap, pieces)
            fwd_m[d] = one_hot(hits)

    for d in range(2):
        tail = jnp.zeros((chunks, cap - OUTER, 2 * HD), BF16)

        @pl.when(z != (2, 1)[d])
        def _():
            inc[:, d, OUTER:] = tail

        @pl.when(z != (1, 2)[d])
        def _():
            rin[:, d, OUTER:] = tail

    @pl.when(~has_left)
    def _():
        inc[:, 0] = jnp.zeros(inc.shape[:1] + inc.shape[2:], BF16)
        rin[:, 1] = jnp.zeros(rin.shape[:1] + rin.shape[2:], BF16)

    @pl.when(~has_right)
    def _():
        inc[:, 1] = jnp.zeros(inc.shape[:1] + inc.shape[2:], BF16)
        rin[:, 0] = jnp.zeros(rin.shape[:1] + rin.shape[2:], BF16)

    def build_slots():
        for e in range(4):
            yy, s = flip(y, e // 2), 1 - flip(core, e % 2)
            i = 2 * z + yy
            at = slice(e * DEC_MAX, (e + 1) * DEC_MAX)
            for j in range(ZS - 1):
                zs = j + jnp.where(j >= z, 1, 0)
                n = zs * 2 + s
                d6 = jnp.where(zs < z, 0, 6)
                column = seg[d6 + IN_AT, n] + pre[n, i] - seg[d6 + IN_FROM, n]
                within = iota((DEC_MAX, cap), 0)
                hits = iota((DEC_MAX, cap), 1) - within == column
                hits = hits & (within < pre[n, i + 1] - pre[n, i])
                slot_m[j, at] = one_hot(hits)
            n = z * 2 + s
            column = s * dec_count + pre[n, i]
            within = iota((DEC_MAX, 2 * dec_count), 0)
            hits = iota((DEC_MAX, 2 * dec_count), 1) - within == column
            hits = hits & (within < pre[n, i + 1] - pre[n, i])
            ownslot_m[at] = one_hot(hits)

    def build_examples():
        for t in range(PARTNERS):
            ey, j = t // ZS, t % ZS
            zs = z if j == ZS - 1 else j + jnp.where(j >= z, 1, 0)
            reader = section_of(zs, flip(y, ey), 1 - core)
            start, begin, size = jnp.int32(0), jnp.int32(0), jnp.int32(0)
            for i in range(PARTNERS):
                length = enc_len[i, me]
                match = readers[i, me] == reader
                begin = jnp.where(match, start, begin)
                size = jnp.where(match, length, size)
                start = start + length
            meta[0, t] = begin
            meta[1, t] = size
        mem_f[:, :, enc_count:] = jnp.zeros((2, 2, ENC_MAX, HD), F32)
        pieces = [(meta[0, t], meta[1, t], t * ENC_MAX) for t in range(PARTNERS)]
        goal = goal_of(enc_count, pieces)
        for b in range(enc_count // 256):
            at = slice(b * 256, (b + 1) * 256)
            grad_m[at, :] = one_hot(iota((256, PARTNERS * ENC_MAX), 1) == goal[at])

    remote = (ZS - 1) * 4 * DEC_MAX

    def build_returns():
        for d in range(2):
            pieces = []
            for n in range(2 * ZS):
                zs, s = n // 2, n % 2
                valid = part(d, IN_LEN, n) > 0
                shift = part(d, IN_AT, n) - part(d, IN_FROM, n)
                j = zs - jnp.where(zs > z, 1, 0)
                ec = lax.rem(1 - s - core + 2, 2)
                for yy in range(2):
                    e = lax.rem(yy - y + 2, 2) * 2 + ec
                    begin = pre[n, 2 * z + yy]
                    length = jnp.where(valid, pre[n, 2 * z + yy + 1] - begin, 0)
                    pieces.append((shift + begin, length, (j * 4 + e) * DEC_MAX))
                begin = pre[n, 2 * z + 2] if d == 0 else jnp.int32(0)
                length = dec_count - begin if d == 0 else pre[n, 2 * z]
                column = remote + part(d, OUT_AT, n)
                pieces.append((shift + begin, jnp.where(valid, length, 0), column))

            @pl.when((has_left, has_right)[d])
            def _():
                hits = iota((cap, remote + cap), 1) == goal_of(cap, pieces)
                ret_m[d] = one_hot(hits)

        pieces = []
        local = 4 * DEC_MAX
        for s in range(2):
            n = z * 2 + s
            ec = lax.rem(1 - s - core + 2, 2)
            for yy in range(2):
                e = lax.rem(yy - y + 2, 2) * 2 + ec
                begin = pre[n, 2 * z + yy]
                length = pre[n, 2 * z + yy + 1] - begin
                pieces.append((s * dec_count + begin, length, e * DEC_MAX))
            begin = pre[n, 2 * z + 2]
            at = s * dec_count
            pieces.append((at + begin, dec_count - begin, local + seg[OUT_AT, n]))
            pieces.append((at, pre[n, 2 * z], local + cap + seg[6 + OUT_AT, n]))
        count = 2 * dec_count
        fin_m[...] = one_hot(iota((count, local + 2 * cap), 1) == goal_of(count, pieces))

    def forward(k, d, starts):
        ring = lax.rem(k, RING)

        @pl.when(k >= RING)
        def _():
            forward_copy(k - RING, d).wait_send()

        @pl.when(jnp.logical_not(starts))
        def _():
            forward_copy(k, d, True).wait_recv()
            block = matmul(fwd_m[d, :, :cap], inc[k, d], NN)
            block = block + matmul(fwd_m[d, :, cap:], own[k], NN)
            out[ring, d] = block.astype(BF16)

        @pl.when(starts)
        def _():
            out[ring, d] = matmul(fwd_m[d, :, cap:], own[k], NN).astype(BF16)

        forward_copy(k, d).start()

    def deliver(k):
        ring = lax.rem(k, RING)

        @pl.when(z == ZS - 1)
        def _():
            forward_copy(k, 0, True).wait_recv()

        @pl.when(z == 0)
        def _():
            forward_copy(k, 1, True).wait_recv()

        @pl.when(k >= RING)
        def _():
            for e in range(1, 4):
                deliver_copy(k - RING, e).wait_send()

        for j in range(ZS - 1):
            d = jnp.where(j < z, 0, 1)
            block = matmul(slot_m[j], inc[k, d], NN).astype(BF16)
            dsend[ring, j] = block.reshape(4, DEC_MAX, 2 * HD)
        block = matmul(ownslot_m[...], own[k], NN).astype(BF16)
        dsend[ring, ZS - 1] = block.reshape(4, DEC_MAX, 2 * HD)
        for e in (3, 2, 1, 0):
            deliver_copy(k, e).start()

    def attend(k):
        ring = lax.rem(k, RING)
        pair = lax.rem(k, 2)
        for ec in range(2):
            memory_copy(k, ec).wait()
        for a in range(2):
            for ec in range(2):
                at = slice(ec * HD, (ec + 1) * HD)
                mem_f[a, ec, :enc_count] = mem_v[pair, a, :, at].astype(F32)

        @pl.when(k + 2 < chunks)
        def _():
            for ec in range(2):
                memory_copy(k + 2, ec).start()

        @pl.when(k >= RING)
        def _():
            for e in range(1, 4):
                answer_copy(k - RING, e).wait_send()

        for e in range(4):
            arrive(deliver_copy(k, e), e)

        @pl.loop(0, 2)
        def _(ey):
            units = [(ey * ZS + j, j, ec) for j in range(ZS) for ec in range(2)]
            column = iota((DEC_MAX, ENC_MAX), 1)

            def tokens(unit, a):
                t, j, ec = unit
                return drecv[k, j, ey * 2 + ec, :, a * HD : (a + 1) * HD]

            def example(unit, a):
                t, j, ec = unit
                return mem_f[a, ec, pl.ds(meta[0, t], ENC_MAX)].astype(BF16)

            keys = [example(unit, 0) for unit in units]
            values = [example(unit, 1) for unit in units]
            scores = [matmul(tokens(u, 0), key, NT) for u, key in zip(units, keys)]
            dprobs = [matmul(tokens(u, 1), value, NT) for u, value in zip(units, values)]
            scores = [jnp.where(column < meta[1, u[0]], s, -jnp.inf) for u, s in zip(units, scores)]
            most = [jnp.max(s, axis=1, keepdims=True) for s in scores]
            weights = [jnp.exp((s - m) * scaling) for s, m in zip(scores, most)]
            scale = [1.0 / jnp.sum(w, axis=1, keepdims=True) for w in weights]
            probs = [w * r for w, r in zip(weights, scale)]
            delta = [jnp.sum(w * d, axis=1, keepdims=True) for w, d in zip(probs, dprobs)]
            low = [w.astype(BF16) for w in probs]
            dscores = [
                (w * (d - e)).astype(BF16) for w, d, e in zip(probs, dprobs, delta)
            ]
            for i, (t, j, ec) in enumerate(units):
                e = ey * 2 + ec
                at = slice(ec * HD, (ec + 1) * HD)
                osend[ring, j, e, :, :HD] = matmul(low[i], values[i], NN).astype(BF16)
                block = matmul(dscores[i], keys[i], NN) * scaling
                osend[ring, j, e, :, HD:] = block.astype(BF16)
                block = matmul(dscores[i], tokens(units[i], 0), TN) * scaling
                d_x[0, t, :, at] = block.astype(BF16)
                d_x[1, t, :, at] = matmul(low[i], tokens(units[i], 1), TN).astype(BF16)

        for e in (3, 2, 1, 0):
            answer_copy(k, e).start()

    def collect(k):
        pair = lax.rem(k, 2)

        @pl.when(k >= 2)
        def _():
            for ec in range(2):
                gradient_copy(k - 2, ec).wait()

        for a in range(2):

            @pl.loop(0, enc_count // 256)
            def _(b):
                at = pl.ds(pl.multiple_of(b * 256, 256), 256)
                block = d_x[a].reshape(PARTNERS * ENC_MAX, 2 * HD)
                mg_v[pair, a, at] = matmul(grad_m[at, :], block, NN).astype(BF16)

        for ec in range(2):
            gradient_copy(k, ec).start()

    def answers(k):
        for e in range(4):
            arrive(answer_copy(k, e), e)

    def give_back(k, d, starts):
        ring = lax.rem(k, RING)

        @pl.when(k >= RING)
        def _():
            return_copy(k - RING, d).wait_send()

        answered = oret[k, : ZS - 1].reshape(remote, 2 * HD)

        @pl.when(jnp.logical_not(starts))
        def _():
            return_copy(k, d, True).wait_recv()
            block = matmul(ret_m[d, :, :remote], answered, NN)
            block = block + matmul(ret_m[d, :, remote:], rin[k, d], NN)
            rout[ring, d] = block.astype(BF16)

        @pl.when(starts)
        def _():
            rout[ring, d] = matmul(ret_m[d, :, :remote], answered, NN).astype(BF16)

        return_copy(k, d).start()

    def finish(k):
        @pl.when(z == 0)
        def _():
            return_copy(k, 0, True).wait_recv()

        @pl.when(z == ZS - 1)
        def _():
            return_copy(k, 1, True).wait_recv()

        local = 4 * DEC_MAX
        block = matmul(fin_m[:, :local], oret[k, ZS - 1].reshape(local, 2 * HD), NN)
        for d in range(2):
            at = local + d * cap
            block = block + matmul(fin_m[:, at : at + cap], rin[k, d], NN)
        fin_v[k] = block.astype(BF16)
        for e in (3, 2, 1, 0):
            for a in range(2):
                last_copy(k, e, a).start()

    for k in range(2):
        for ec in range(2):
            memory_copy(k, ec).start()

    near = ZS - 1
    lag = 1
    back = lag * near + 2
    settled = lag * far + jnp.where(far < near, 3, 2)
    steps = chunks + back + lag * near

    def during(k, condition=None):
        go = (k >= 0) & (k < chunks)
        if condition is not None:
            go = go & condition
        return pl.when(go)

    @pl.loop(0, steps)
    def _(t):
        @during(t)
        def _():
            for e in range(4):
                for a in range(2):
                    arrive(exchange_copy(t, e, a), e)

            @pl.when(t + 2 < chunks)
            def _():
                exchange(t + 2)

        @during(t - lag * z, has_right)
        def _():
            forward(t - lag * z, 0, z == 0)

        @during(t - lag * (near - z), has_left)
        def _():
            forward(t - lag * (near - z), 1, z == near)

        @pl.when(t == 0)
        def _():
            build_slots()
            build_examples()
            build_returns()

        @during(t - lag * far)
        def _():
            deliver(t - lag * far)

        @during(t - settled)
        def _():
            answers(t - settled)

        @during(t - back - lag * (near - z), has_left)
        def _():
            give_back(t - back - lag * (near - z), 0, z == near)

        @during(t - back - lag * z, has_right)
        def _():
            give_back(t - back - lag * z, 1, z == 0)

        @during(t - lag * far - 1)
        def _():
            attend(t - lag * far - 1)

        @during(t - lag * far - 1)
        def _():
            collect(t - lag * far - 1)

        @during(t - back - lag * far)
        def _():
            finish(t - back - lag * far)

    @pl.loop(0, chunks)
    def _(k):
        for e in range(4):
            for a in range(2):
                if e == 0:
                    last_copy(k, e, a).wait()
                else:
                    exchange_copy(k, e, a).wait_send()
                    last_copy(k, e, a).wait_send()
                    last_arrival(k, e, a).wait_recv()

    @pl.loop(chunks - RING, chunks)
    def _(k):
        for e in range(1, 4):
            deliver_copy(k, e).wait_send()
            answer_copy(k, e).wait_send()

        @pl.when(has_right)
        def _():
            forward_copy(k, 0).wait_send()
            return_copy(k, 1).wait_send()

        @pl.when(has_left)
        def _():
            forward_copy(k, 1).wait_send()
            return_copy(k, 0).wait_send()

    @pl.loop(chunks - 2, chunks)
    def _(k):
        for ec in range(2):
            gradient_copy(k, ec).wait()


def packed_body(memory, queries, out_grad, enc_lengths, dec_lengths, readers):
    enc_count, width = memory.shape[1:]
    rows = queries.shape[0]
    count = 4 * rows
    chunks = width // 2 // HD
    pair = 2 * HD
    scalars = (enc_lengths.T, dec_lengths.T, readers.T)
    anywhere = pl.BlockSpec(memory_space=pl.ANY)
    dma = pltpu.SemaphoreType.DMA
    blocks = (ZS, 4, DEC_MAX, pair)
    local = 4 * DEC_MAX
    remote = (ZS - 1) * local

    def vmem(*shape):
        return pltpu.VMEM(shape, BF16)

    return pl.pallas_call(
        packed_kernel,
        out_shape=(
            jax.ShapeDtypeStruct(queries.shape, BF16),
            jax.ShapeDtypeStruct(queries.shape, BF16),
            jax.ShapeDtypeStruct(memory.shape, BF16),
        ),
        in_specs=[anywhere] * 6,
        out_specs=(anywhere,) * 3,
        scratch_shapes=[
            vmem(chunks, count, pair),
            vmem(chunks, 2, CAP, pair),
            vmem(RING, 2, CAP, pair),
            vmem(RING, *blocks),
            vmem(chunks, *blocks),
            vmem(RING, *blocks),
            vmem(chunks, *blocks),
            vmem(chunks, 2, CAP, pair),
            vmem(RING, 2, CAP, pair),
            vmem(chunks, count, pair),
            vmem(2, 2, enc_count, pair),
            vmem(2, 2, enc_count, pair),
            pltpu.VMEM((2, 2, enc_count + ENC_MAX, HD), F32),
            vmem(2, PARTNERS, ENC_MAX, pair),
            vmem(2, CAP, CAP + count),
            vmem(ZS - 1, local, CAP),
            vmem(local, count),
            vmem(2, CAP, remote + CAP),
            vmem(count, local + 2 * CAP),
            vmem(enc_count, PARTNERS * ENC_MAX),
            *[pltpu.SMEM(array.shape, jnp.int32) for array in scalars],
            pltpu.SMEM((2 * ZS, PARTNERS + 1), jnp.int32),
            pltpu.SMEM((12, 2 * ZS), jnp.int32),
            pltpu.SMEM((2, PARTNERS), jnp.int32),
            dma((chunks, 4, 2)),
            dma((chunks, 4, 2)),
            dma((RING, 2)),
            dma((chunks, 2)),
            dma((RING, 4)),
            dma((chunks, 4)),
            dma((RING, 4)),
            dma((chunks, 4)),
            dma((RING, 2)),
            dma((chunks, 2)),
            dma((chunks, 4, 2)),
            dma((chunks, 4, 2)),
            dma((2, 2)),
            dma((2, 2)),
            dma((3,)),
        ],
        compiler_params=pltpu.CompilerParams(
            collective_id=1, has_side_effects=True, vmem_limit_bytes=60 * 1024 * 1024
        ),
    )(memory, queries, out_grad, *scalars)


def fits(dec_lengths):
    place = np.arange(2 * ZS * 2 * 2 * ZS).reshape(4 * ZS, 2 * ZS)
    source, half = place // (8 * ZS), place // (4 * ZS) % 2
    goal = place % (2 * ZS) // 2
    blocks = []
    cuts = np.repeat(np.arange(1, ZS), 4)
    for cut in range(1, ZS):
        for y in range(2):
            blocks.append((half == y) & (source < cut) & (goal >= cut))
            blocks.append((half == y) & (source >= cut) & (goal < cut))
    counts = jnp.where(np.stack(blocks), dec_lengths, 0)
    most = np.array([CAP if cut == ZS // 2 else OUTER for cut in cuts])
    return jnp.all(jnp.sum(counts, axis=(1, 2)) <= most)


def body(sections, tensors, *args):
    packs = (sections, tensors) == (4 * ZS, 2)
    padded = functools.partial(padded_body, sections, tensors, packs)
    if not packs:
        return padded(*args)
    return lax.cond(fits(args[4]), packed_body, padded, *args)


def solution(mesh):
    placed = (
        P(None, "section", "tensor"),
        P(("section", "tensor"), None),
        P(("section", "tensor"), None),
        P(),
        P(),
        P(),
    )
    return jax.shard_map(
        functools.partial(body, mesh.shape["section"], mesh.shape["tensor"]),
        mesh=mesh,
        in_specs=placed,
        out_specs=(
            P(("section", "tensor"), None),
            P(("section", "tensor"), None),
            P(None, "section", "tensor"),
        ),
        check_vma=False,
    )
```

```python
import functools

import jax
import jax.numpy as jnp
import numpy as np
from jax import lax
from jax.experimental import pallas as pl
from jax.experimental.pallas import tpu as pltpu
from jax.sharding import PartitionSpec as P

HD = 128
ENC_MAX = 128
DEC_MAX = 64
PARTNERS = 8
MOST_CHUNKS = 8
BF16 = jnp.bfloat16
F32 = jnp.float32
MESH = pl.DeviceIdType.MESH


def matmul(a, b, dims):
    return lax.dot_general(a, b, (dims, ((), ())), preferred_element_type=F32)


NN = ((1,), (0,))
NT = ((1,), (1,))
TN = ((0,), (0,))


def chunk_count(width):
    return min(MOST_CHUNKS, width // HD)


def staged_kernel(sections, tensors, *refs):
    inputs, results, staging = refs[:6], refs[6:9], refs[9:12]
    sem = refs[-1]
    kernel(sections, tensors, *inputs, *staging, *refs[12:-1])
    copies = [
        pltpu.make_async_copy(source, target, sem.at[i])
        for i, (source, target) in enumerate(zip(staging, results))
    ]
    for copy in copies:
        copy.start()
    for copy in copies:
        copy.wait()


def kernel(
    sections,
    tensors,
    mem_hbm,
    q_hbm,
    g_hbm,
    enc_hbm,
    dec_hbm,
    readers_hbm,
    att_out,
    qg_out,
    mg_out,
    mem_v,
    dec_v,
    fsend,
    frecv,
    osend,
    oret,
    fin_v,
    kv_x,
    d_x,
    pack_m,
    unpack_m,
    enc_m,
    grad_m,
    enc_len,
    dec_len,
    readers,
    meta,
    a_send,
    a_recv,
    a_local,
    f_send,
    f_recv,
    o_send,
    o_recv,
    g_send,
    g_recv,
    g_local,
    m_in,
    s_in,
):
    me = lax.axis_index("section")
    mine = lax.axis_index("tensor")
    rows = q_hbm.shape[0]
    enc_count = mem_v.shape[1]
    dec_count = dec_v.shape[2]
    width = mem_v.shape[2]
    chunks = chunk_count(width)
    piece = width // chunks
    spacing = sections // PARTNERS
    scaling = HD ** (-0.5)

    def holder_of(slot):
        return lax.rem(me + 2 * sections - slot * spacing - 1, sections)

    def reader_of(slot):
        return lax.rem(me + slot * spacing + 1, sections)

    half = PARTNERS // 2

    def peer_of(step):
        return lax.rem(mine + step, tensors)

    mem_copy = pltpu.make_async_copy(mem_hbm, mem_v, m_in)
    scalar_copies = [
        pltpu.make_async_copy(source, target, s_in.at[i])
        for i, (source, target) in enumerate(
            ((enc_hbm, enc_len), (dec_hbm, dec_len), (readers_hbm, readers))
        )
    ]
    for copy in scalar_copies:
        copy.start()

    barrier = pltpu.get_barrier_semaphore()
    for step in range(1, tensors):
        pl.semaphore_signal(
            barrier, inc=1, device_id={"tensor": peer_of(step)}, device_id_type=MESH
        )
    for slot in range(PARTNERS):
        pl.semaphore_signal(
            barrier, inc=1, device_id={"section": holder_of(slot)}, device_id_type=MESH
        )
        pl.semaphore_signal(
            barrier, inc=1, device_id={"section": reader_of(slot)}, device_id_type=MESH
        )
    pl.semaphore_wait(barrier, tensors - 1 + 2 * PARTNERS)

    own_rows = pl.ds(pl.multiple_of(mine * rows, rows), rows)

    def first_copy(c, a, step):
        peer = peer_of(step)
        source = (q_hbm, g_hbm)[a]
        columns = pl.ds(pl.multiple_of(peer * width + c * piece, piece), piece)
        if step == 0:
            return pltpu.make_async_copy(
                source.at[:, columns], dec_v.at[c, a, own_rows], a_local.at[c, a]
            )
        return pltpu.make_async_remote_copy(
            src_ref=source.at[:, columns],
            dst_ref=dec_v.at[c, a, own_rows],
            send_sem=a_send.at[c, a, step - 1],
            recv_sem=a_recv.at[c, a, step - 1],
            device_id={"tensor": peer},
            device_id_type=MESH,
        )

    def fetch(c):
        for a in range(2):
            for step in list(range(1, tensors)) + [0]:
                first_copy(c, a, step).start()

    fetch(0)
    mem_copy.start()
    for copy in scalar_copies:
        copy.wait()

    start = jnp.int32(0)
    for i in range(PARTNERS):
        length = dec_len[i, me]
        meta[0, i] = start
        meta[1, i] = length
        start = start + length
    for slot in range(PARTNERS):
        reader = reader_of(slot)
        start, begin, size = jnp.int32(0), jnp.int32(0), jnp.int32(0)
        for j in range(PARTNERS):
            length = enc_len[j, me]
            match = readers[j, me] == reader
            begin = jnp.where(match, start, begin)
            size = jnp.where(match, length, size)
            start = start + length
        meta[2, slot] = begin
        meta[3, slot] = size

    def one_hot(hits):
        return jnp.where(hits, 1.0, 0.0).astype(BF16)

    def iota(shape, dim):
        return lax.broadcasted_iota(jnp.int32, shape, dim)

    for i in range(PARTNERS):
        shape = (DEC_MAX, dec_count)
        within = iota(shape, 0)
        hits = (iota(shape, 1) - within == meta[0, i]) & (within < meta[1, i])
        pack_m[i // half, (i % half) * DEC_MAX : (i % half + 1) * DEC_MAX, :] = one_hot(hits)

    def forward_copy(c, slot):
        holder = holder_of(slot)
        return pltpu.make_async_remote_copy(
            src_ref=fsend.at[c, :, lax.div(holder, spacing)],
            dst_ref=frecv.at[c, :, slot],
            send_sem=f_send.at[c, slot],
            recv_sem=f_recv.at[c, slot],
            device_id={"section": holder},
            device_id_type=MESH,
        )

    def back_copy(c, slot):
        return pltpu.make_async_remote_copy(
            src_ref=osend.at[c, :, slot],
            dst_ref=oret.at[c, :, lax.div(me, spacing)],
            send_sem=o_send.at[c, slot],
            recv_sem=o_recv.at[c, lax.div(me, spacing)],
            device_id={"section": reader_of(slot)},
            device_id_type=MESH,
        )

    def back_arrival(c, i):
        return pltpu.make_async_remote_copy(
            src_ref=osend.at[c, :, i],
            dst_ref=oret.at[c, :, i],
            send_sem=o_send.at[c, i],
            recv_sem=o_recv.at[c, i],
            device_id={"section": reader_of(i)},
            device_id_type=MESH,
        )

    def last_copy(c, a, step):
        peer = peer_of(step)
        target = (att_out, qg_out)[a]
        source = fin_v.at[c, a, pl.ds(pl.multiple_of(peer * rows, rows), rows)]
        columns = pl.ds(pl.multiple_of(mine * width + c * piece, piece), piece)
        if step == 0:
            return pltpu.make_async_copy(source, target.at[:, columns], g_local.at[c, a])
        return pltpu.make_async_remote_copy(
            src_ref=source,
            dst_ref=target.at[:, columns],
            send_sem=g_send.at[c, a, step - 1],
            recv_sem=g_recv.at[c, a, step - 1],
            device_id={"tensor": peer},
            device_id_type=MESH,
        )

    def pack(c):
        for a in range(2):
            first_copy(c, a, 0).wait()
            for step in range(1, tensors):
                first_copy(c, a, step).wait_recv()
        if c + 1 < chunks:
            fetch(c + 1)
        for a in range(2):
            for g in range(2):
                block = matmul(pack_m[g], dec_v[c, a], NN).astype(BF16)
                fsend[c, a, g * half : (g + 1) * half] = block.reshape(half, DEC_MAX, piece)

        @pl.loop(0, PARTNERS)
        def _(turn):
            forward_copy(c, turn).start()

    def expand(c):
        @pl.loop(0, PARTNERS // 2)
        def _(g):
            for a in range(2):
                block = matmul(enc_m[g], mem_v[a, :, c * piece : (c + 1) * piece], NN)
                kv_x[c, a, pl.ds(g * 2, 2)] = block.astype(BF16).reshape(2, ENC_MAX, piece)

    def attend(c):
        @pl.loop(0, PARTNERS)
        def _(turn):
            slot = turn
            forward_copy(c, slot).wait_recv()
            valid = iota((DEC_MAX, ENC_MAX), 1) < meta[3, slot]
            for h in range(piece // HD):
                at = slice(h * HD, (h + 1) * HD)
                q = frecv[c, 0, slot, :, at]
                g = frecv[c, 1, slot, :, at]
                k = kv_x[c, 0, slot, :, at]
                v = kv_x[c, 1, slot, :, at]
                scores = jnp.where(valid, matmul(q, k, NT) * scaling, -jnp.inf)
                weights = jnp.exp(scores - jnp.max(scores, axis=1, keepdims=True))
                probs = weights / jnp.sum(weights, axis=1, keepdims=True)
                low = probs.astype(BF16)
                dprobs = matmul(g, v, NT)
                delta = jnp.sum(probs * dprobs, axis=1, keepdims=True)
                dscores = (probs * (dprobs - delta)).astype(BF16)
                osend[c, 0, slot, :, at] = matmul(low, v, NN).astype(BF16)
                osend[c, 1, slot, :, at] = (matmul(dscores, k, NN) * scaling).astype(BF16)
                d_x[0, slot, :, at] = (matmul(dscores, q, TN) * scaling).astype(BF16)
                d_x[1, slot, :, at] = matmul(low, g, TN).astype(BF16)
            back_copy(c, slot).start()

    def collect(c):
        @pl.loop(0, enc_count // 256)
        def _(b):
            at = pl.ds(pl.multiple_of(b * 256, 256), 256)
            for a in range(2):
                block = d_x[a].reshape(PARTNERS * ENC_MAX, piece)
                mg_out[a, at, c * piece : (c + 1) * piece] = matmul(
                    grad_m[at, :], block, NN
                ).astype(BF16)

    def finish(c):
        @pl.loop(0, PARTNERS)
        def _(i):
            back_arrival(c, i).wait_recv()

        for a in range(2):
            block = oret[c, a].reshape(PARTNERS * DEC_MAX, piece)
            fin_v[c, a] = matmul(unpack_m[...], block, NN).astype(BF16)
            for step in list(range(1, tensors)) + [0]:
                last_copy(c, a, step).start()

    def settle():
        for c in range(chunks):
            for a in range(2):
                for step in range(1, tensors):
                    first_copy(c, a, step).wait_send()

            @pl.loop(0, PARTNERS)
            def _(slot):
                forward_copy(c, slot).wait_send()
                back_copy(c, slot).wait_send()

    pack(0)

    for slot in range(PARTNERS):
        shape = (ENC_MAX, enc_count)
        within = iota(shape, 0)
        hits = (iota(shape, 1) - within == meta[2, slot]) & (within < meta[3, slot])
        enc_m[slot // 2, (slot % 2) * ENC_MAX : (slot % 2 + 1) * ENC_MAX, :] = one_hot(hits)
    mem_copy.wait()
    expand(0)
    pack(1)

    position = iota((dec_count, 1), 0)
    goal = jnp.full((dec_count, 1), -1, jnp.int32)
    for i in range(PARTNERS):
        within = position - meta[0, i]
        goal = jnp.where((within >= 0) & (within < meta[1, i]), within + i * DEC_MAX, goal)
    unpack_m[...] = one_hot(iota((dec_count, PARTNERS * DEC_MAX), 1) == goal)
    for b in range(enc_count // 256):
        position = iota((256, 1), 0) + b * 256
        goal = jnp.full((256, 1), -1, jnp.int32)
        for slot in range(PARTNERS):
            within = position - meta[2, slot]
            goal = jnp.where(
                (within >= 0) & (within < meta[3, slot]), within + slot * ENC_MAX, goal
            )
        hits = iota((256, PARTNERS * ENC_MAX), 1) == goal
        grad_m[b * 256 : (b + 1) * 256, :] = one_hot(hits)

    expand(1)
    for c in range(2, chunks):
        pack(c)
        expand(c)
    for c in range(chunks):
        attend(c)
        collect(c)
        if c >= 3:
            finish(c - 3)
    for c in range(max(chunks - 3, 0), chunks):
        if c == chunks - 1:
            settle()
        finish(c)

    for c in range(chunks):
        for a in range(2):
            for step in range(1, tensors):
                last_copy(c, a, step).wait()
            last_copy(c, a, 0).wait()


def padded_body(sections, tensors, staged, memory, queries, out_grad, enc_lengths, dec_lengths, readers):
    enc_count, width = memory.shape[1:]
    rows = queries.shape[0]
    dec_count = rows * tensors
    chunks = chunk_count(width)
    piece = width // chunks
    blocks = (chunks, 2, PARTNERS, DEC_MAX, piece)
    peers = max(tensors - 1, 1)
    scalars = (enc_lengths.T, dec_lengths.T, readers.T)
    anywhere = pl.BlockSpec(memory_space=pl.ANY)
    resident = pl.BlockSpec(memory_space=pltpu.VMEM)
    results = [array.shape for array in (queries, queries, memory)]
    dma = pltpu.SemaphoreType.DMA
    return pl.pallas_call(
        functools.partial(staged_kernel if staged else kernel, sections, tensors),
        out_shape=tuple(
            jax.ShapeDtypeStruct(shape, BF16) if staged else pltpu.VMEM(shape, BF16)
            for shape in results
        ),
        in_specs=[anywhere] * 6,
        out_specs=(anywhere if staged else resident,) * 3,
        scratch_shapes=[
            *[pltpu.VMEM(shape, BF16) for shape in results if staged],
            pltpu.VMEM((2, enc_count, width), BF16),
            pltpu.VMEM((chunks, 2, dec_count, piece), BF16),
            pltpu.VMEM(blocks, BF16),
            pltpu.VMEM(blocks, BF16),
            pltpu.VMEM(blocks, BF16),
            pltpu.VMEM(blocks, BF16),
            pltpu.VMEM((chunks, 2, dec_count, piece), BF16),
            pltpu.VMEM((chunks, 2, PARTNERS, ENC_MAX, piece), BF16),
            pltpu.VMEM((2, PARTNERS, ENC_MAX, piece), BF16),
            pltpu.VMEM((2, PARTNERS // 2 * DEC_MAX, dec_count), BF16),
            pltpu.VMEM((dec_count, PARTNERS * DEC_MAX), BF16),
            pltpu.VMEM((PARTNERS // 2, 2 * ENC_MAX, enc_count), BF16),
            pltpu.VMEM((enc_count, PARTNERS * ENC_MAX), BF16),
            *[pltpu.SMEM(array.shape, jnp.int32) for array in scalars],
            pltpu.SMEM((4, PARTNERS), jnp.int32),
            dma((chunks, 2, peers)),
            dma((chunks, 2, peers)),
            dma((chunks, 2)),
            dma((chunks, PARTNERS)),
            dma((chunks, PARTNERS)),
            dma((chunks, PARTNERS)),
            dma((chunks, PARTNERS)),
            dma((chunks, 2, peers)),
            dma((chunks, 2, peers)),
            dma((chunks, 2)),
            dma,
            dma((3,)),
            *[dma((3,))] * staged,
        ],
        compiler_params=pltpu.CompilerParams(
            collective_id=0, has_side_effects=True, vmem_limit_bytes=(56 if staged else 46) * 1024 * 1024
        ),
    )(memory, queries, out_grad, *scalars)


ZS = 4
CAP = 640
OUTER = 544


class Hop:
    def __init__(self, make, middle):
        self.make, self.middle = make, middle

    def each(self, action):
        @pl.when(self.middle)
        def _():
            action(self.make(CAP))

        @pl.when(jnp.logical_not(self.middle))
        def _():
            action(self.make(OUTER))

    def start(self):
        self.each(lambda copy: copy.start())

    def wait_send(self):
        self.each(lambda copy: copy.wait_send())

    def wait_recv(self):
        self.each(lambda copy: copy.wait_recv())


RING = 4


def packed_kernel(
    mem_hbm,
    q_hbm,
    g_hbm,
    enc_hbm,
    dec_hbm,
    readers_hbm,
    att_out,
    qg_out,
    mg_out,
    own,
    inc,
    out,
    dsend,
    drecv,
    osend,
    oret,
    rin,
    rout,
    fin_v,
    mem_v,
    mg_v,
    mem_f,
    d_x,
    fwd_m,
    slot_m,
    ownslot_m,
    ret_m,
    fin_m,
    grad_m,
    enc_len,
    dec_len,
    readers,
    pre,
    seg,
    meta,
    a_send,
    a_recv,
    f_send,
    f_recv,
    d_send,
    d_recv,
    o_send,
    o_recv,
    r_send,
    r_recv,
    g_send,
    g_recv,
    m_in,
    m_out,
    s_in,
):
    me = lax.axis_index("section")
    x = lax.axis_index("tensor")
    z = lax.div(me, 4)
    y = lax.rem(lax.div(me, 2), 2)
    core = lax.rem(me, 2)
    rows = q_hbm.shape[0]
    dec_count = 2 * rows
    enc_count = mem_hbm.shape[1]
    width = mem_hbm.shape[2]
    half_width = width // 2
    chunks = half_width // HD
    cap = inc.shape[2]
    scaling = HD ** (-0.5)
    has_right = z < ZS - 1
    has_left = z > 0
    far = jnp.maximum(z, ZS - 1 - z)

    def flip(value, step):
        return lax.rem(value + step, 2)

    def section_of(zz, yy, cc):
        return zz * 4 + yy * 2 + cc

    def iota(shape, dim):
        return lax.broadcasted_iota(jnp.int32, shape, dim)

    def one_hot(hits):
        return jnp.where(hits, 1.0, 0.0).astype(BF16)

    scalar_copies = [
        pltpu.make_async_copy(source, target, s_in.at[i])
        for i, (source, target) in enumerate(
            ((enc_hbm, enc_len), (dec_hbm, dec_len), (readers_hbm, readers))
        )
    ]
    for copy in scalar_copies:
        copy.start()

    barrier = pltpu.get_barrier_semaphore()

    def greet(section, tensor):
        pl.semaphore_signal(
            barrier,
            inc=1,
            device_id={"section": section, "tensor": tensor},
            device_id_type=MESH,
        )

    greet(section_of(z, y, core), flip(x, 1))
    greet(section_of(z, y, flip(core, 1)), flip(x, 1))
    for e in range(1, 4):
        greet(section_of(z, flip(y, e // 2), flip(core, e % 2)), x)

    @pl.when(has_right)
    def _():
        greet(me + 4, x)

    @pl.when(has_left)
    def _():
        greet(me - 4, x)

    pl.semaphore_wait(barrier, 5 + jnp.where(has_right, 1, 0) + jnp.where(has_left, 1, 0))

    def exchange_copy(k, e, a):
        to_core = flip(core, e // 2)
        to_x = flip(x, e % 2)
        source = (q_hbm, g_hbm)[a]
        column = to_x * width + to_core * half_width + k * HD
        start = core * dec_count + x * rows
        args = (
            source.at[:, pl.ds(pl.multiple_of(column, HD), HD)],
            own.at[k, pl.ds(pl.multiple_of(start, rows), rows), a * HD : (a + 1) * HD],
        )
        if e == 0:
            return pltpu.make_async_copy(*args, a_recv.at[k, e, a])
        return pltpu.make_async_remote_copy(
            src_ref=args[0],
            dst_ref=args[1],
            send_sem=a_send.at[k, e, a],
            recv_sem=a_recv.at[k, e, a],
            device_id={"section": section_of(z, y, to_core), "tensor": to_x},
            device_id_type=MESH,
        )

    def exchange(k):
        for e in (3, 2, 1, 0):
            for a in range(2):
                exchange_copy(k, e, a).start()

    def memory_copy(k, ec):
        column = flip(core, ec) * half_width + k * HD
        ring = lax.rem(k, 2)
        return pltpu.make_async_copy(
            mem_hbm.at[:, :, pl.ds(pl.multiple_of(column, HD), HD)],
            mem_v.at[ring, :, :, ec * HD : (ec + 1) * HD],
            m_in.at[ring, ec],
        )

    def gradient_copy(k, ec):
        column = flip(core, ec) * half_width + k * HD
        ring = lax.rem(k, 2)
        return pltpu.make_async_copy(
            mg_v.at[ring, :, :, ec * HD : (ec + 1) * HD],
            mg_out.at[:, :, pl.ds(pl.multiple_of(column, HD), HD)],
            m_out.at[ring, ec],
        )

    def forward_copy(k, d, arrives=False):
        ring = lax.rem(k, RING)

        def make(count):
            return pltpu.make_async_remote_copy(
                src_ref=out.at[ring, d, :count],
                dst_ref=inc.at[k, d, :count],
                send_sem=f_send.at[ring, d],
                recv_sem=f_recv.at[k, d],
                device_id={"section": me + (4, -4)[d]},
                device_id_type=MESH,
            )

        return Hop(make, (z == 1, z == 2)[d ^ arrives])

    def return_copy(k, d, arrives=False):
        ring = lax.rem(k, RING)

        def make(count):
            return pltpu.make_async_remote_copy(
                src_ref=rout.at[ring, d, :count],
                dst_ref=rin.at[k, d, :count],
                send_sem=r_send.at[ring, d],
                recv_sem=r_recv.at[k, d],
                device_id={"section": me + (-4, 4)[d]},
                device_id_type=MESH,
            )

        return Hop(make, (z == 2, z == 1)[d ^ arrives])

    def slot_copy(send, recv, send_sem, recv_sem, k, e):
        ring = lax.rem(k, RING)
        if e == 0:
            return pltpu.make_async_copy(
                send.at[ring, :, e], recv.at[k, :, e], recv_sem.at[k, e]
            )
        return pltpu.make_async_remote_copy(
            src_ref=send.at[ring, :, e],
            dst_ref=recv.at[k, :, e],
            send_sem=send_sem.at[ring, e],
            recv_sem=recv_sem.at[k, e],
            device_id={"section": section_of(z, flip(y, e // 2), flip(core, e % 2))},
            device_id_type=MESH,
        )

    deliver_copy = functools.partial(slot_copy, dsend, drecv, d_send, d_recv)
    answer_copy = functools.partial(slot_copy, osend, oret, o_send, o_recv)

    def arrive(copy, e):
        if e == 0:
            copy.wait()
        else:
            copy.wait_recv()

    def last_copy(k, e, a):
        to_core = flip(core, e // 2)
        to_x = flip(x, e % 2)
        column = x * width + core * half_width + k * HD
        start = to_core * dec_count + to_x * rows
        args = (
            fin_v.at[k, pl.ds(pl.multiple_of(start, rows), rows), a * HD : (a + 1) * HD],
            (att_out, qg_out)[a].at[:, pl.ds(pl.multiple_of(column, HD), HD)],
        )
        if e == 0:
            return pltpu.make_async_copy(*args, g_recv.at[k, e, a])
        return pltpu.make_async_remote_copy(
            src_ref=args[0],
            dst_ref=args[1],
            send_sem=g_send.at[k, e, a],
            recv_sem=g_recv.at[k, e, a],
            device_id={"section": section_of(z, y, to_core), "tensor": to_x},
            device_id_type=MESH,
        )

    def last_arrival(k, e, a):
        from_core = flip(core, e // 2)
        from_x = flip(x, e % 2)
        column = from_x * width + from_core * half_width + k * HD
        start = core * dec_count + x * rows
        return pltpu.make_async_remote_copy(
            src_ref=fin_v.at[
                k, pl.ds(pl.multiple_of(start, rows), rows), a * HD : (a + 1) * HD
            ],
            dst_ref=(att_out, qg_out)[a].at[:, pl.ds(pl.multiple_of(column, HD), HD)],
            send_sem=g_send.at[k, e, a],
            recv_sem=g_recv.at[k, e, a],
            device_id={"section": section_of(z, y, from_core), "tensor": from_x},
            device_id_type=MESH,
        )

    for k in range(2):
        exchange(k)
    for copy in scalar_copies:
        copy.wait()

    for n in range(2 * ZS):
        source = section_of(n // 2, y, n % 2)
        start = jnp.int32(0)
        for i in range(PARTNERS):
            pre[n, i] = start
            start = start + dec_len[i, source]
        pre[n, PARTNERS] = start

    OUT_LEN, OUT_AT, OUT_FROM, IN_LEN, IN_AT, IN_FROM = range(6)
    for d in range(2):
        out_at, in_at = jnp.int32(0), jnp.int32(0)
        for n in range(2 * ZS):
            zs = n // 2
            if d == 0:
                begin = pre[n, 2 * z + 2]
                out_len = jnp.where(zs <= z, dec_count - begin, 0)
                first = pre[n, 2 * z]
                in_len = jnp.where(zs < z, dec_count - first, 0)
            else:
                begin, first = jnp.int32(0), jnp.int32(0)
                out_len = jnp.where(zs >= z, pre[n, 2 * z], 0)
                in_len = jnp.where(zs > z, pre[n, 2 * z + 2], 0)
            for name, value in (
                (OUT_LEN, out_len),
                (OUT_AT, out_at),
                (OUT_FROM, begin),
                (IN_LEN, in_len),
                (IN_AT, in_at),
                (IN_FROM, first),
            ):
                seg[d * 6 + name, n] = value
            out_at, in_at = out_at + out_len, in_at + in_len

    def part(d, name, n):
        return seg[d * 6 + name, n]

    def goal_of(count, pieces):
        position = iota((count, 1), 0)
        goal = jnp.full((count, 1), -1, jnp.int32)
        for at, length, column in pieces:
            within = position - at
            goal = jnp.where((within >= 0) & (within < length), within + column, goal)
        return goal

    for d in range(2):
        pieces = []
        for n in range(2 * ZS):
            zs, s = n // 2, n % 2
            column = jnp.where(
                zs == z,
                cap + s * dec_count + part(d, OUT_FROM, n),
                part(d, IN_AT, n) + part(d, OUT_FROM, n) - part(d, IN_FROM, n),
            )
            pieces.append((part(d, OUT_AT, n), part(d, OUT_LEN, n), column))

        @pl.when((has_right, has_left)[d])
        def _():
            hits = iota((cap, cap + 2 * dec_count), 1) == goal_of(cap, pieces)
            fwd_m[d] = one_hot(hits)

    for d in range(2):
        tail = jnp.zeros((chunks, cap - OUTER, 2 * HD), BF16)

        @pl.when(z != (2, 1)[d])
        def _():
            inc[:, d, OUTER:] = tail

        @pl.when(z != (1, 2)[d])
        def _():
            rin[:, d, OUTER:] = tail

    @pl.when(~has_left)
    def _():
        inc[:, 0] = jnp.zeros(inc.shape[:1] + inc.shape[2:], BF16)
        rin[:, 1] = jnp.zeros(rin.shape[:1] + rin.shape[2:], BF16)

    @pl.when(~has_right)
    def _():
        inc[:, 1] = jnp.zeros(inc.shape[:1] + inc.shape[2:], BF16)
        rin[:, 0] = jnp.zeros(rin.shape[:1] + rin.shape[2:], BF16)

    def build_slots():
        for e in range(4):
            yy, s = flip(y, e // 2), 1 - flip(core, e % 2)
            i = 2 * z + yy
            at = slice(e * DEC_MAX, (e + 1) * DEC_MAX)
            for j in range(ZS - 1):
                zs = j + jnp.where(j >= z, 1, 0)
                n = zs * 2 + s
                d6 = jnp.where(zs < z, 0, 6)
                column = seg[d6 + IN_AT, n] + pre[n, i] - seg[d6 + IN_FROM, n]
                within = iota((DEC_MAX, cap), 0)
                hits = iota((DEC_MAX, cap), 1) - within == column
                hits = hits & (within < pre[n, i + 1] - pre[n, i])
                slot_m[j, at] = one_hot(hits)
            n = z * 2 + s
            column = s * dec_count + pre[n, i]
            within = iota((DEC_MAX, 2 * dec_count), 0)
            hits = iota((DEC_MAX, 2 * dec_count), 1) - within == column
            hits = hits & (within < pre[n, i + 1] - pre[n, i])
            ownslot_m[at] = one_hot(hits)

    def build_examples():
        for t in range(PARTNERS):
            ey, j = t // ZS, t % ZS
            zs = z if j == ZS - 1 else j + jnp.where(j >= z, 1, 0)
            reader = section_of(zs, flip(y, ey), 1 - core)
            start, begin, size = jnp.int32(0), jnp.int32(0), jnp.int32(0)
            for i in range(PARTNERS):
                length = enc_len[i, me]
                match = readers[i, me] == reader
                begin = jnp.where(match, start, begin)
                size = jnp.where(match, length, size)
                start = start + length
            meta[0, t] = begin
            meta[1, t] = size
        mem_f[:, :, enc_count:] = jnp.zeros((2, 2, ENC_MAX, HD), F32)
        pieces = [(meta[0, t], meta[1, t], t * ENC_MAX) for t in range(PARTNERS)]
        goal = goal_of(enc_count, pieces)
        for b in range(enc_count // 256):
            at = slice(b * 256, (b + 1) * 256)
            grad_m[at, :] = one_hot(iota((256, PARTNERS * ENC_MAX), 1) == goal[at])

    remote = (ZS - 1) * 4 * DEC_MAX

    def build_returns():
        for d in range(2):
            pieces = []
            for n in range(2 * ZS):
                zs, s = n // 2, n % 2
                valid = part(d, IN_LEN, n) > 0
                shift = part(d, IN_AT, n) - part(d, IN_FROM, n)
                j = zs - jnp.where(zs > z, 1, 0)
                ec = lax.rem(1 - s - core + 2, 2)
                for yy in range(2):
                    e = lax.rem(yy - y + 2, 2) * 2 + ec
                    begin = pre[n, 2 * z + yy]
                    length = jnp.where(valid, pre[n, 2 * z + yy + 1] - begin, 0)
                    pieces.append((shift + begin, length, (j * 4 + e) * DEC_MAX))
                begin = pre[n, 2 * z + 2] if d == 0 else jnp.int32(0)
                length = dec_count - begin if d == 0 else pre[n, 2 * z]
                column = remote + part(d, OUT_AT, n)
                pieces.append((shift + begin, jnp.where(valid, length, 0), column))

            @pl.when((has_left, has_right)[d])
            def _():
                hits = iota((cap, remote + cap), 1) == goal_of(cap, pieces)
                ret_m[d] = one_hot(hits)

        pieces = []
        local = 4 * DEC_MAX
        for s in range(2):
            n = z * 2 + s
            ec = lax.rem(1 - s - core + 2, 2)
            for yy in range(2):
                e = lax.rem(yy - y + 2, 2) * 2 + ec
                begin = pre[n, 2 * z + yy]
                length = pre[n, 2 * z + yy + 1] - begin
                pieces.append((s * dec_count + begin, length, e * DEC_MAX))
            begin = pre[n, 2 * z + 2]
            at = s * dec_count
            pieces.append((at + begin, dec_count - begin, local + seg[OUT_AT, n]))
            pieces.append((at, pre[n, 2 * z], local + cap + seg[6 + OUT_AT, n]))
        count = 2 * dec_count
        fin_m[...] = one_hot(iota((count, local + 2 * cap), 1) == goal_of(count, pieces))

    def forward(k, d, starts):
        ring = lax.rem(k, RING)

        @pl.when(k >= RING)
        def _():
            forward_copy(k - RING, d).wait_send()

        @pl.when(jnp.logical_not(starts))
        def _():
            forward_copy(k, d, True).wait_recv()
            block = matmul(fwd_m[d, :, :cap], inc[k, d], NN)
            block = block + matmul(fwd_m[d, :, cap:], own[k], NN)
            out[ring, d] = block.astype(BF16)

        @pl.when(starts)
        def _():
            out[ring, d] = matmul(fwd_m[d, :, cap:], own[k], NN).astype(BF16)

        forward_copy(k, d).start()

    def deliver(k):
        ring = lax.rem(k, RING)

        @pl.when(z == ZS - 1)
        def _():
            forward_copy(k, 0, True).wait_recv()

        @pl.when(z == 0)
        def _():
            forward_copy(k, 1, True).wait_recv()

        @pl.when(k >= RING)
        def _():
            for e in range(1, 4):
                deliver_copy(k - RING, e).wait_send()

        for j in range(ZS - 1):
            d = jnp.where(j < z, 0, 1)
            block = matmul(slot_m[j], inc[k, d], NN).astype(BF16)
            dsend[ring, j] = block.reshape(4, DEC_MAX, 2 * HD)
        block = matmul(ownslot_m[...], own[k], NN).astype(BF16)
        dsend[ring, ZS - 1] = block.reshape(4, DEC_MAX, 2 * HD)
        for e in (3, 2, 1, 0):
            deliver_copy(k, e).start()

    def attend(k):
        ring = lax.rem(k, RING)
        pair = lax.rem(k, 2)
        for ec in range(2):
            memory_copy(k, ec).wait()
        for a in range(2):
            for ec in range(2):
                at = slice(ec * HD, (ec + 1) * HD)
                mem_f[a, ec, :enc_count] = mem_v[pair, a, :, at].astype(F32)

        @pl.when(k + 2 < chunks)
        def _():
            for ec in range(2):
                memory_copy(k + 2, ec).start()

        @pl.when(k >= RING)
        def _():
            for e in range(1, 4):
                answer_copy(k - RING, e).wait_send()

        for e in range(4):
            arrive(deliver_copy(k, e), e)

        @pl.loop(0, 2)
        def _(ey):
            units = [(ey * ZS + j, j, ec) for j in range(ZS) for ec in range(2)]
            column = iota((DEC_MAX, ENC_MAX), 1)

            def tokens(unit, a):
                t, j, ec = unit
                return drecv[k, j, ey * 2 + ec, :, a * HD : (a + 1) * HD]

            def example(unit, a):
                t, j, ec = unit
                return mem_f[a, ec, pl.ds(meta[0, t], ENC_MAX)].astype(BF16)

            keys = [example(unit, 0) for unit in units]
            values = [example(unit, 1) for unit in units]
            scores = [matmul(tokens(u, 0), key, NT) for u, key in zip(units, keys)]
            dprobs = [matmul(tokens(u, 1), value, NT) for u, value in zip(units, values)]
            scores = [jnp.where(column < meta[1, u[0]], s, -jnp.inf) for u, s in zip(units, scores)]
            most = [jnp.max(s, axis=1, keepdims=True) for s in scores]
            weights = [jnp.exp((s - m) * scaling) for s, m in zip(scores, most)]
            scale = [1.0 / jnp.sum(w, axis=1, keepdims=True) for w in weights]
            probs = [w * r for w, r in zip(weights, scale)]
            delta = [jnp.sum(w * d, axis=1, keepdims=True) for w, d in zip(probs, dprobs)]
            low = [w.astype(BF16) for w in probs]
            dscores = [
                (w * (d - e)).astype(BF16) for w, d, e in zip(probs, dprobs, delta)
            ]
            for i, (t, j, ec) in enumerate(units):
                e = ey * 2 + ec
                at = slice(ec * HD, (ec + 1) * HD)
                osend[ring, j, e, :, :HD] = matmul(low[i], values[i], NN).astype(BF16)
                block = matmul(dscores[i], keys[i], NN) * scaling
                osend[ring, j, e, :, HD:] = block.astype(BF16)
                block = matmul(dscores[i], tokens(units[i], 0), TN) * scaling
                d_x[0, t, :, at] = block.astype(BF16)
                d_x[1, t, :, at] = matmul(low[i], tokens(units[i], 1), TN).astype(BF16)

        for e in (3, 2, 1, 0):
            answer_copy(k, e).start()

    def collect(k):
        pair = lax.rem(k, 2)

        @pl.when(k >= 2)
        def _():
            for ec in range(2):
                gradient_copy(k - 2, ec).wait()

        for a in range(2):
            block = d_x[a].reshape(PARTNERS * ENC_MAX, 2 * HD)
            mg_v[pair, a] = matmul(grad_m[...], block, NN).astype(BF16)

        for ec in range(2):
            gradient_copy(k, ec).start()

    def answers(k):
        for e in range(4):
            arrive(answer_copy(k, e), e)

    def give_back(k, d, starts):
        ring = lax.rem(k, RING)

        @pl.when(k >= RING)
        def _():
            return_copy(k - RING, d).wait_send()

        answered = oret[k, : ZS - 1].reshape(remote, 2 * HD)

        @pl.when(jnp.logical_not(starts))
        def _():
            return_copy(k, d, True).wait_recv()
            block = matmul(ret_m[d, :, :remote], answered, NN)
            block = block + matmul(ret_m[d, :, remote:], rin[k, d], NN)
            rout[ring, d] = block.astype(BF16)

        @pl.when(starts)
        def _():
            rout[ring, d] = matmul(ret_m[d, :, :remote], answered, NN).astype(BF16)

        return_copy(k, d).start()

    def finish(k):
        @pl.when(z == 0)
        def _():
            return_copy(k, 0, True).wait_recv()

        @pl.when(z == ZS - 1)
        def _():
            return_copy(k, 1, True).wait_recv()

        local = 4 * DEC_MAX
        block = matmul(fin_m[:, :local], oret[k, ZS - 1].reshape(local, 2 * HD), NN)
        for d in range(2):
            at = local + d * cap
            block = block + matmul(fin_m[:, at : at + cap], rin[k, d], NN)
        fin_v[k] = block.astype(BF16)
        for e in (3, 2, 1, 0):
            for a in range(2):
                last_copy(k, e, a).start()

    for k in range(2):
        for ec in range(2):
            memory_copy(k, ec).start()

    near = ZS - 1
    lag = 1
    back = lag * near + 2
    settled = lag * far + jnp.where(far < near, 3, 2)
    steps = chunks + back + lag * near

    def during(k, condition=None):
        go = (k >= 0) & (k < chunks)
        if condition is not None:
            go = go & condition
        return pl.when(go)

    @pl.loop(0, steps)
    def _(t):
        @during(t)
        def _():
            for e in range(4):
                for a in range(2):
                    arrive(exchange_copy(t, e, a), e)

            @pl.when(t + 2 < chunks)
            def _():
                exchange(t + 2)

        @during(t - lag * z, has_right)
        def _():
            forward(t - lag * z, 0, z == 0)

        @during(t - lag * (near - z), has_left)
        def _():
            forward(t - lag * (near - z), 1, z == near)

        @pl.when(t == 0)
        def _():
            build_slots()
            build_examples()
            build_returns()

        @during(t - lag * far)
        def _():
            deliver(t - lag * far)

        @during(t - settled)
        def _():
            answers(t - settled)

        @during(t - back - lag * (near - z), has_left)
        def _():
            give_back(t - back - lag * (near - z), 0, z == near)

        @during(t - back - lag * z, has_right)
        def _():
            give_back(t - back - lag * z, 1, z == 0)

        @during(t - lag * far - 1)
        def _():
            attend(t - lag * far - 1)

        @during(t - lag * far - 1)
        def _():
            collect(t - lag * far - 1)

        @during(t - back - lag * far)
        def _():
            finish(t - back - lag * far)

    @pl.loop(0, chunks)
    def _(k):
        for e in range(4):
            for a in range(2):
                if e == 0:
                    last_copy(k, e, a).wait()
                else:
                    exchange_copy(k, e, a).wait_send()
                    last_copy(k, e, a).wait_send()
                    last_arrival(k, e, a).wait_recv()

    @pl.loop(chunks - RING, chunks)
    def _(k):
        for e in range(1, 4):
            deliver_copy(k, e).wait_send()
            answer_copy(k, e).wait_send()

        @pl.when(has_right)
        def _():
            forward_copy(k, 0).wait_send()
            return_copy(k, 1).wait_send()

        @pl.when(has_left)
        def _():
            forward_copy(k, 1).wait_send()
            return_copy(k, 0).wait_send()

    @pl.loop(chunks - 2, chunks)
    def _(k):
        for ec in range(2):
            gradient_copy(k, ec).wait()


def packed_body(memory, queries, out_grad, enc_lengths, dec_lengths, readers):
    enc_count, width = memory.shape[1:]
    rows = queries.shape[0]
    count = 4 * rows
    chunks = width // 2 // HD
    pair = 2 * HD
    scalars = (enc_lengths.T, dec_lengths.T, readers.T)
    anywhere = pl.BlockSpec(memory_space=pl.ANY)
    dma = pltpu.SemaphoreType.DMA
    blocks = (ZS, 4, DEC_MAX, pair)
    local = 4 * DEC_MAX
    remote = (ZS - 1) * local

    def vmem(*shape):
        return pltpu.VMEM(shape, BF16)

    return pl.pallas_call(
        packed_kernel,
        out_shape=(
            jax.ShapeDtypeStruct(queries.shape, BF16),
            jax.ShapeDtypeStruct(queries.shape, BF16),
            jax.ShapeDtypeStruct(memory.shape, BF16),
        ),
        in_specs=[anywhere] * 6,
        out_specs=(anywhere,) * 3,
        scratch_shapes=[
            vmem(chunks, count, pair),
            vmem(chunks, 2, CAP, pair),
            vmem(RING, 2, CAP, pair),
            vmem(RING, *blocks),
            vmem(chunks, *blocks),
            vmem(RING, *blocks),
            vmem(chunks, *blocks),
            vmem(chunks, 2, CAP, pair),
            vmem(RING, 2, CAP, pair),
            vmem(chunks, count, pair),
            vmem(2, 2, enc_count, pair),
            vmem(2, 2, enc_count, pair),
            pltpu.VMEM((2, 2, enc_count + ENC_MAX, HD), F32),
            vmem(2, PARTNERS, ENC_MAX, pair),
            vmem(2, CAP, CAP + count),
            vmem(ZS - 1, local, CAP),
            vmem(local, count),
            vmem(2, CAP, remote + CAP),
            vmem(count, local + 2 * CAP),
            vmem(enc_count, PARTNERS * ENC_MAX),
            *[pltpu.SMEM(array.shape, jnp.int32) for array in scalars],
            pltpu.SMEM((2 * ZS, PARTNERS + 1), jnp.int32),
            pltpu.SMEM((12, 2 * ZS), jnp.int32),
            pltpu.SMEM((2, PARTNERS), jnp.int32),
            dma((chunks, 4, 2)),
            dma((chunks, 4, 2)),
            dma((RING, 2)),
            dma((chunks, 2)),
            dma((RING, 4)),
            dma((chunks, 4)),
            dma((RING, 4)),
            dma((chunks, 4)),
            dma((RING, 2)),
            dma((chunks, 2)),
            dma((chunks, 4, 2)),
            dma((chunks, 4, 2)),
            dma((2, 2)),
            dma((2, 2)),
            dma((3,)),
        ],
        compiler_params=pltpu.CompilerParams(
            collective_id=1, has_side_effects=True, vmem_limit_bytes=60 * 1024 * 1024
        ),
    )(memory, queries, out_grad, *scalars)


def fits(dec_lengths):
    place = np.arange(2 * ZS * 2 * 2 * ZS).reshape(4 * ZS, 2 * ZS)
    source, half = place // (8 * ZS), place // (4 * ZS) % 2
    goal = place % (2 * ZS) // 2
    blocks = []
    cuts = np.repeat(np.arange(1, ZS), 4)
    for cut in range(1, ZS):
        for y in range(2):
            blocks.append((half == y) & (source < cut) & (goal >= cut))
            blocks.append((half == y) & (source >= cut) & (goal < cut))
    counts = jnp.where(np.stack(blocks), dec_lengths, 0)
    most = np.array([CAP if cut == ZS // 2 else OUTER for cut in cuts])
    return jnp.all(jnp.sum(counts, axis=(1, 2)) <= most)


def body(sections, tensors, *args):
    packs = (sections, tensors) == (4 * ZS, 2)
    padded = functools.partial(padded_body, sections, tensors, packs)
    if not packs:
        return padded(*args)
    return lax.cond(fits(args[4]), packed_body, padded, *args)


def solution(mesh):
    placed = (
        P(None, "section", "tensor"),
        P(("section", "tensor"), None),
        P(("section", "tensor"), None),
        P(),
        P(),
        P(),
    )
    return jax.shard_map(
        functools.partial(body, mesh.shape["section"], mesh.shape["tensor"]),
        mesh=mesh,
        in_specs=placed,
        out_specs=(
            P(("section", "tensor"), None),
            P(("section", "tensor"), None),
            P(None, "section", "tensor"),
        ),
        check_vma=False,
    )
```
